32 devices in a mesh: layout: 2 (over x), tile: 16 (over z, y, core).
Axes of the slice: x: 2, y: 2, z: 4, core: 2. Of those that a mesh axis runs over, the one named last changes fastest.
Arguments:
- velocity: float32 [2, 3, 4, 512, 256], P('layout', None, None, 'tile'), may hold values from -1.2 to 2.2, as said below
- inflow: float32 [2, 3, 4, 256], P('layout'), may hold values from -1.2 to 2.2, as said below
- turbine_site: int32 [2, 40], P('layout'), may hold values from 0 to 47, as said below
- turbine_block: int32 [2, 40], P('layout'), may hold values from 0 to 63, as said below
- turbine_slot: int32 [2, 40], P('layout'), may hold values from 0 to 47, as said below
- smear: float32 [2, 48, 512], P('layout', 'tile'), may hold values from 0.2 to 2
- yaw: float32 [2, 48], P('layout', 'tile'), may hold values from -0.5 to 0.5
- thrust_coef: float32 [2, 48], P('layout', 'tile'), may hold values from 0.5 to 1.5
Outputs:
- velocity_out: float32 [2, 3, 4, 512, 256], P('layout', None, None, 'tile')
- slot_power: float32 [2, 48], P('layout', 'tile')
The draws below stay inside these ranges and needn't reach their ends.
Inputs may be any that keep to these rules, and one draw needn't show every extreme that they name: `turbine_site`: within a layout all sites differ; the tile of site s is s // 3; in every layout some tile holds exactly 3 turbines. `turbine_block`: blocks are numbered x-block times (8) plus y-block; turbines of one tile have different blocks. `turbine_slot`: within a layout all slots differ; the owner tile of slot s is s // 3; in every layout some tile owns exactly 3 turbines; slots that no turbine names are empty. `velocity`: component 0 lies within 1 - 1.2 and 1 + 1.2, components 1 and 2 within -1.2 and 1.2. `inflow`: component 0 lies within 1 - 1.2 and 1 + 1.2, components 1 and 2 within -1.2 and 1.2.
All inputs are finite; a program needn't handle non-finite values.
Results may differ from the reference program's by a relative error of at most 0.0003.
Values sent between devices are 32-bit elements; how exact they have to be, the bound alone decides.
A program may use at most 64 MiB of HBM per device.

```python
import math
import jax
import jax.numpy as jnp
from jax import lax

CX = 32
NY = 256
LEV = 4
TURB = 40
BX = 4
BY = 32
HOME_MOST = 3
OWN_SLOTS = 3
LAYOUTS = 2
NX = 512
STEPS = 2
BLK = 512
BLOCKS = 64
SITES = 48
SLOTS = 48


def velocity_law(key, shape):
    component = lax.broadcasted_iota(jnp.int32, shape, 1)
    mean_part = jnp.where(component == 0, 1.0, 0.0).astype(jnp.float32)
    noise_part = 0.4 * jax.random.truncated_normal(key, -3.0, 3.0, shape, jnp.float32)
    return mean_part + noise_part


def draw_velocity(key, part):
    return velocity_law(jax.random.fold_in(key, 11), (LAYOUTS, 3, LEV, NX, NY))


def draw_inflow(key, part):
    return velocity_law(jax.random.fold_in(key, 13), (STEPS, 3, LEV, NY))


def distinct_fill(key, group_size, slot_total):
    key_perm, key_order = jax.random.split(key)
    shuffled = jax.random.permutation(key_perm, slot_total).astype(jnp.int32)
    full_group = shuffled[0] // group_size
    ordering = jnp.argsort(jnp.arange(slot_total, dtype=jnp.int32) + slot_total * (shuffled // group_size == full_group).astype(jnp.int32), stable=True)
    remaining = shuffled[ordering]
    leading = full_group * group_size + jnp.arange(group_size, dtype=jnp.int32)
    chosen = jnp.concatenate([leading, remaining[:TURB - group_size]])
    mixing = jax.random.permutation(key_order, TURB).astype(jnp.int32)
    return chosen[mixing]


def one_layout_lists(key):
    key_site = jax.random.fold_in(key, 1)
    key_slot = jax.random.fold_in(key, 2)
    key_shift = jax.random.fold_in(key, 3)
    key_offset = jax.random.fold_in(key, 4)
    site_list = distinct_fill(key_site, HOME_MOST, SITES)
    slot_list = distinct_fill(key_slot, OWN_SLOTS, SLOTS)
    home_tile = site_list // HOME_MOST
    home_rank = site_list % HOME_MOST
    rank_span = BLOCKS // HOME_MOST
    tile_shift = jax.random.randint(key_shift, (SITES // HOME_MOST,), 0, BLOCKS, jnp.int32)
    offset = jax.random.randint(key_offset, (TURB,), 0, rank_span, jnp.int32)
    block_list = (home_rank * rank_span + offset + tile_shift[home_tile]) % BLOCKS
    return (site_list, block_list.astype(jnp.int32), slot_list)


def layout_lists(key):
    layout_keys = jax.random.split(jax.random.fold_in(key, 7), LAYOUTS)
    return jax.vmap(one_layout_lists)(layout_keys)


def draw_turbine_site(key, part):
    return layout_lists(key)[0]


def draw_turbine_block(key, part):
    return layout_lists(key)[1]


def draw_turbine_slot(key, part):
    return layout_lists(key)[2]


def block_scale(stream_key, extent, pieces, smallest, largest):
    factor_of, own = 1.0, jax.random.fold_in(stream_key, 6)
    for position, shards_of in pieces:
        steps = jnp.exp(jax.random.uniform(jax.random.fold_in(own, position), (shards_of,), jnp.float32, smallest / len(pieces), largest / len(pieces)))
        factor_of = factor_of * jnp.repeat(steps, extent[position] // shards_of).reshape([-1 if axis == position else 1 for axis in range(len(extent))])
    return factor_of


def setup_inputs(seed: int = 0) -> dict:
    keys = jax.random.split(jax.random.key(seed), 9)
    velocity = draw_velocity(jax.random.fold_in(keys[8], 71), 0)
    inflow = draw_inflow(jax.random.fold_in(keys[8], 71), 0)
    turbine_site = draw_turbine_site(jax.random.fold_in(keys[8], 71), 0)
    turbine_block = draw_turbine_block(jax.random.fold_in(keys[8], 71), 0)
    turbine_slot = draw_turbine_slot(jax.random.fold_in(keys[8], 71), 0)
    smear = jnp.clip(jnp.exp(math.log(2.0) - 2.3025851 * jax.random.uniform(keys[5], (LAYOUTS, SLOTS, BLK), jnp.float32) ** block_scale(keys[5], (LAYOUTS, SLOTS, BLK), ((0, 2), (1, 16)), -0.2, 0.2)), 0.2, 2.0)
    yaw = jnp.clip(jax.random.uniform(keys[6], (LAYOUTS, SLOTS), jnp.float32, -0.5, 0.5) * block_scale(keys[6], (LAYOUTS, SLOTS), ((0, 2), (1, 16)), -0.4, 0.0), -0.5, 0.5)
    thrust_coef = jnp.clip(0.5 + 1.0 * jax.random.uniform(keys[7], (LAYOUTS, SLOTS), jnp.float32) ** block_scale(keys[7], (LAYOUTS, SLOTS), ((0, 2), (1, 16)), -0.2, 0.2), 0.5, 1.5)
    return {"velocity": velocity, "inflow": inflow, "turbine_site": turbine_site, "turbine_block": turbine_block, "turbine_slot": turbine_slot, "smear": smear, "yaw": yaw, "thrust_coef": thrust_coef}


time_step = 0.1
smag_coef = 0.0256
strain_floor = 0.01

def advance(x_padded):
    wrapped = jnp.concatenate([x_padded[..., -1:], x_padded, x_padded[..., :1]], axis=3)
    padded = jnp.concatenate([wrapped[:, :1], wrapped, wrapped[:, -1:]], axis=1)
    centre = padded[:, 1:-1, 1:-1, 1:-1]
    x_minus = padded[:, 1:-1, :-2, 1:-1]
    x_plus = padded[:, 1:-1, 2:, 1:-1]
    y_minus = padded[:, 1:-1, 1:-1, :-2]
    y_plus = padded[:, 1:-1, 1:-1, 2:]
    z_minus = padded[:, :-2, 1:-1, 1:-1]
    z_plus = padded[:, 2:, 1:-1, 1:-1]
    grad_x = 0.5 * (x_plus - x_minus)
    grad_y = 0.5 * (y_plus - y_minus)
    grad_z = 0.5 * (z_plus - z_minus)
    shear_xy = grad_y[0] + grad_x[1]
    shear_xz = grad_z[0] + grad_x[2]
    shear_yz = grad_z[1] + grad_y[2]
    strain_sq = 2.0 * (grad_x[0] * grad_x[0] + grad_y[1] * grad_y[1] + grad_z[2] * grad_z[2])
    strain_sq = strain_sq + shear_xy * shear_xy + shear_xz * shear_xz + shear_yz * shear_yz
    viscosity = smag_coef * jnp.sqrt(strain_sq + strain_floor)
    laplace = x_plus + x_minus + y_plus + y_minus + z_plus + z_minus - 6.0 * centre
    along_x = centre[0]
    along_y = centre[1]
    along_z = centre[2]
    upwind = jnp.maximum(along_x, 0.0) * (centre - x_minus) + jnp.minimum(along_x, 0.0) * (x_plus - centre)
    upwind = upwind + jnp.maximum(along_y, 0.0) * (centre - y_minus) + jnp.minimum(along_y, 0.0) * (y_plus - centre)
    upwind = upwind + jnp.maximum(along_z, 0.0) * (centre - z_minus) + jnp.minimum(along_z, 0.0) * (z_plus - centre)
    return centre + time_step * (viscosity * laplace - upwind)

def rotor_forces(blocks, weights, angles, thrust_coefs, present):
    cosine = jnp.cos(angles)[:, None]
    sine_part = jnp.sin(angles)[:, None]
    normal = blocks[:, 0] * cosine + blocks[:, 1] * sine_part
    weight_sum = jnp.where(present, lax.optimization_barrier(jnp.sum(weights, axis=1)), 1.0)
    disk_speed = lax.optimization_barrier(jnp.sum(weights * normal, axis=1)) / weight_sum
    thrust = -0.5 * thrust_coefs * disk_speed * jnp.abs(disk_speed)
    spread = thrust[:, None] * weights
    forces = jnp.stack([spread * cosine, spread * sine_part], axis=1)
    powers = 0.5 * thrust_coefs * jnp.abs(disk_speed) * disk_speed * disk_speed
    return (forces, powers)

def reference(velocity, inflow, turbine_site, turbine_block, turbine_slot, smear, yaw, thrust_coef):
    y_blocks = NY // BY

    def one_layout(operands):
        current, site_list, blocks_of, slot_list, weights, angles, thrust_coefs = operands
        power_sum = jnp.zeros((TURB,), jnp.float32)
        for step_index in range(STEPS):
            inflow_now = inflow[step_index]
            x_padded = jnp.concatenate([inflow_now[:, :, None, :], current, current[:, :, -1:]], axis=2)
            stepped = advance(x_padded)
            source = current[:2]

            def one_turbine(spread, turbine):
                home_tile = site_list[turbine] // HOME_MOST
                x_first = (home_tile * CX + blocks_of[turbine] // y_blocks * BX).astype(jnp.int32)
                y_first = (blocks_of[turbine] % y_blocks * BY).astype(jnp.int32)
                zero_index = jnp.zeros((), jnp.int32)
                where_at = (zero_index, zero_index, x_first, y_first)
                disk_cells = lax.dynamic_slice(source, where_at, (2, LEV, BX, BY)).reshape(1, 2, BLK)
                owner_slot = slot_list[turbine]
                forces, powers = rotor_forces(disk_cells, weights[owner_slot][None], angles[owner_slot][None], thrust_coefs[owner_slot][None], jnp.ones((1,), jnp.bool_))
                existing = lax.dynamic_slice(spread, where_at, (2, LEV, BX, BY))
                spread = lax.dynamic_update_slice(spread, existing + forces[0].reshape(2, LEV, BX, BY), where_at)
                return (spread, powers[0])
            spread, powers = lax.scan(one_turbine, jnp.zeros((2, LEV, NX, NY), jnp.float32), jnp.arange(TURB, dtype=jnp.int32))
            current = jnp.concatenate([stepped[:2] + time_step * spread, stepped[2:]], axis=0)
            power_sum = power_sum + powers
        power_out = jnp.zeros((SLOTS,), jnp.float32).at[slot_list].set(power_sum / STEPS)
        return (current, power_out)
    return lax.map(one_layout, (velocity, turbine_site, turbine_block, turbine_slot, smear, yaw, thrust_coef))
```

```python
import functools

import jax
import jax.numpy as jnp
from jax import lax
from jax.experimental import pallas as pl
from jax.experimental.pallas import tpu as pltpu
from jax.sharding import PartitionSpec as P

BX = 4
BY = 32
HOME_MOST = 3
OWN_SLOTS = 3
LANES = 128
ROWS = 8

TIME_STEP = 0.1
SMAG = 0.0256
FLOOR = 0.01

MESH = pl.DeviceIdType.MESH


def kernel(
    tiles, layouts, levels, width_x, halves, turbines,
    vel_ref, inflow_ref, site_ref, block_ref, slot_ref, smear_ref, yaw_ref, coef_ref,
    out_ref, power_ref,
    q, site_s, block_s, slot_s, smear_v, yaw_v, coef_v, gathered, weights_v,
    planes, edge_out, edge_in, powers, power_v,
    local_sem, gather_send, gather_recv, plane_send, plane_recv,
    edge_send, edge_recv, power_send, power_recv,
):
    tile = lax.axis_index("tile")
    layout = lax.axis_index("layout")
    steps = layouts
    fields = 3 * levels
    x_tiles = width_x // ROWS
    first = ROWS
    y_blocks = halves * LANES // BY
    segs = LANES // BY

    def tile_at(distance):
        return lax.rem(tile + distance, tiles)

    def layout_at(distance):
        return lax.rem(layout + distance, layouts)

    barrier = pltpu.get_barrier_semaphore()
    for d in range(1, tiles):
        pl.semaphore_signal(
            barrier, inc=1, device_id=(layout, tile_at(d)), device_id_type=MESH
        )
    for d in range(1, layouts):
        pl.semaphore_signal(
            barrier, inc=1, device_id=(layout_at(d), tile), device_id_type=MESH
        )

    loads = [
        pltpu.make_async_copy(smear_ref.at[0], smear_v, local_sem.at[0]),
        pltpu.make_async_copy(yaw_ref, yaw_v, local_sem.at[1]),
        pltpu.make_async_copy(coef_ref, coef_v, local_sem.at[2]),
    ]
    field_loads = [
        pltpu.make_async_copy(
            vel_ref.at[0, :, :, :, pl.ds(h * LANES, LANES)],
            q.at[0, :, :, h, pl.ds(first, width_x), :],
            local_sem.at[3 + h],
        )
        for h in range(halves)
    ]
    base = 3 + halves
    plane_load = pltpu.make_async_copy(
        inflow_ref.at[0], planes.at[layout], local_sem.at[base]
    )
    list_loads = [
        pltpu.make_async_copy(site_ref, site_s, local_sem.at[base + 1]),
        pltpu.make_async_copy(block_ref, block_s, local_sem.at[base + 2]),
        pltpu.make_async_copy(slot_ref, slot_s, local_sem.at[base + 3]),
    ]
    for copy in loads + field_loads + [plane_load] + list_loads:
        copy.start()

    for copy in loads:
        copy.wait()
    lane1 = lax.broadcasted_iota(jnp.int32, (1, LANES), 1)
    for j in range(OWN_SLOTS):
        total = jnp.zeros((1, 1), jnp.float32)
        for l in range(levels):
            row = smear_v[pl.ds(j, 1), pl.ds(l * LANES, LANES)]
            gathered[tile, pl.ds(j * levels + l, 1), :] = row
            total = total + jnp.sum(row, axis=1, keepdims=True)
        angle = yaw_v[:, j : j + 1]
        packed = jnp.where(lane1 == 0, jnp.cos(angle), 0.0)
        packed = jnp.where(lane1 == 1, jnp.sin(angle), packed)
        packed = jnp.where(lane1 == 2, coef_v[:, j : j + 1], packed)
        packed = jnp.where(lane1 == 3, 1.0 / total, packed)
        gathered[tile, pl.ds(OWN_SLOTS * levels + j, 1), :] = packed

    for copy in field_loads:
        copy.wait()

    def pack_edge(step, side):
        row = first if side == 0 else first + width_x - 1
        for c in range(3):
            for l in range(levels):
                for h in range(halves):
                    i = (c * levels + l) * halves + h
                    edge_out[step, side, pl.ds(i, 1), :] = q[
                        step % 2, c, l, h, pl.ds(row, 1), :
                    ]

    def edge_copy(step, side):
        target = tile - 1 if side == 0 else tile + 1
        return pltpu.make_async_remote_copy(
            src_ref=edge_out.at[step, side],
            dst_ref=edge_in.at[step, 1 - side],
            send_sem=edge_send.at[step, side],
            recv_sem=edge_recv.at[step, 1 - side],
            device_id=(layout, target),
            device_id_type=MESH,
        )

    def send_edges(step):
        @pl.when(tile > 0)
        def _():
            edge_copy(step, 0).start()

        @pl.when(tile < tiles - 1)
        def _():
            edge_copy(step, 1).start()

    pack_edge(0, 0)
    pack_edge(0, 1)
    plane_load.wait()

    pl.semaphore_wait(barrier, tiles - 1 + layouts - 1)

    send_edges(0)

    def plane_copy(d):
        return pltpu.make_async_remote_copy(
            src_ref=planes.at[layout],
            dst_ref=planes.at[layout],
            send_sem=plane_send.at[d],
            recv_sem=plane_recv.at[d],
            device_id=(layout_at(d), tile),
            device_id_type=MESH,
        )

    @pl.when(tile == 0)
    def _():
        for d in range(1, layouts):
            plane_copy(d).start()

    def gather_copy(d):
        return pltpu.make_async_remote_copy(
            src_ref=gathered.at[tile],
            dst_ref=gathered.at[tile],
            send_sem=gather_send.at[d],
            recv_sem=gather_recv.at[d],
            device_id=(layout, tile_at(d)),
            device_id_type=MESH,
        )

    for d in range(1, tiles):
        gather_copy(d).start()

    for copy in list_loads:
        copy.wait()
    home_slot = [jnp.int32(0)] * HOME_MOST
    home_block = [jnp.int32(0)] * HOME_MOST
    home_on = [jnp.int32(0)] * HOME_MOST
    own_site = [jnp.int32(0)] * OWN_SLOTS
    own_on = [jnp.int32(0)] * OWN_SLOTS
    for k in range(turbines):
        site = site_s[0, k]
        block = block_s[0, k]
        slot = slot_s[0, k]
        for j in range(HOME_MOST):
            hit = site == tile * HOME_MOST + j
            home_slot[j] = jnp.where(hit, slot, home_slot[j])
            home_block[j] = jnp.where(hit, block, home_block[j])
            home_on[j] = jnp.where(hit, 1, home_on[j])
        for j in range(OWN_SLOTS):
            hit = slot == tile * OWN_SLOTS + j
            own_site[j] = jnp.where(hit, site, own_site[j])
            own_on[j] = jnp.where(hit, 1, own_on[j])

    lane = lax.broadcasted_iota(jnp.int32, (ROWS, LANES), 1)
    row_id = lax.broadcasted_iota(jnp.int32, (ROWS, LANES), 0)
    lane_seg = lane // BY
    row_in = row_id % BX
    row_half = row_id // BX

    def stencil_tile(src, dst, xt):
        r = first + xt * ROWS
        here = pl.ds(r, ROWS)
        below_rows = pl.ds(r - 1, ROWS)
        above_rows = pl.ds(r + 1, ROWS)
        for l in range(levels):
            centre = [[q[src, c, l, h, here, :] for h in range(halves)] for c in range(3)]
            rolled_m = [
                [pltpu.roll(centre[c][h], 1, 1) for h in range(halves)] for c in range(3)
            ]
            rolled_p = [
                [pltpu.roll(centre[c][h], LANES - 1, 1) for h in range(halves)]
                for c in range(3)
            ]
            for h in range(halves):
                plus, minus = [], []
                for c in range(3):
                    mid = centre[c][h]
                    xm = q[src, c, l, h, below_rows, :]
                    xp = q[src, c, l, h, above_rows, :]
                    ym = jnp.where(lane == 0, rolled_m[c][h - 1], rolled_m[c][h])
                    yp = jnp.where(
                        lane == LANES - 1, rolled_p[c][(h + 1) % halves], rolled_p[c][h]
                    )
                    zm = mid if l == 0 else q[src, c, l - 1, h, here, :]
                    zp = mid if l == levels - 1 else q[src, c, l + 1, h, here, :]
                    plus.append([xp - mid, yp - mid, zp - mid])
                    minus.append([mid - xm, mid - ym, mid - zm])

                def grad(c, a):
                    return plus[c][a] + minus[c][a]

                gxx, gyy, gzz = grad(0, 0), grad(1, 1), grad(2, 2)
                sxy = grad(0, 1) + grad(1, 0)
                sxz = grad(0, 2) + grad(2, 0)
                syz = grad(1, 2) + grad(2, 1)
                strain = 2.0 * (gxx * gxx + gyy * gyy + gzz * gzz)
                strain = strain + sxy * sxy + sxz * sxz + syz * syz + 4.0 * FLOOR
                nu = (0.5 * SMAG * TIME_STEP) * (strain * lax.rsqrt(strain))
                ups, downs = [], []
                for a in range(3):
                    speed = TIME_STEP * centre[a][h]
                    ups.append(nu - jnp.minimum(speed, 0.0))
                    downs.append(nu + jnp.maximum(speed, 0.0))
                for c in range(3):
                    change = ups[0] * plus[c][0] - downs[0] * minus[c][0]
                    change += ups[1] * plus[c][1] - downs[1] * minus[c][1]
                    change += ups[2] * plus[c][2] - downs[2] * minus[c][2]
                    q[dst, c, l, h, here, :] = centre[c][h] + change

    def unpack_edge(step):
        src = step % 2
        left = pl.ds(first - 1, 1)
        right = pl.ds(first + width_x, 1)

        @pl.when(tile > 0)
        def _():
            edge_copy(step, 1).wait_recv()

        def fill(side, rows, value):
            for c in range(3):
                for l in range(levels):
                    for h in range(halves):
                        q[src, c, l, h, rows, :] = value(c, l, h)

        def received(side):
            return lambda c, l, h: edge_in[
                step, side, pl.ds((c * levels + l) * halves + h, 1), :
            ]

        @pl.when(tile > 0)
        def _():
            fill(0, left, received(0))

        @pl.when(tile == 0)
        def _():
            if step == 0:
                for d in range(1, layouts):
                    pltpu.make_async_remote_copy(
                        src_ref=planes.at[layout],
                        dst_ref=planes.at[layout_at(layouts - d)],
                        send_sem=plane_send.at[d],
                        recv_sem=plane_recv.at[d],
                        device_id=(layout_at(d), tile),
                        device_id_type=MESH,
                    ).wait_recv()
            fill(
                0,
                left,
                lambda c, l, h: planes[step, c, pl.ds(l, 1), pl.ds(h * LANES, LANES)],
            )

        @pl.when(tile < tiles - 1)
        def _():
            edge_copy(step, 0).wait_recv()
            fill(1, right, received(1))

        @pl.when(tile == tiles - 1)
        def _():
            fill(
                1,
                right,
                lambda c, l, h: q[src, c, l, h, pl.ds(first + width_x - 1, 1), :],
            )

    place = []
    for j in range(HOME_MOST):
        xb = lax.div(home_block[j], jnp.int32(y_blocks))
        yb = lax.rem(home_block[j], jnp.int32(y_blocks))
        per = ROWS // BX
        place.append(
            (
                lax.div(xb, jnp.int32(per)),
                lax.rem(xb, jnp.int32(per)),
                lax.div(yb, jnp.int32(segs)),
                lax.rem(yb, jnp.int32(segs)),
            )
        )

    def lay_weights():
        params = []
        for j in range(HOME_MOST):
            owner = lax.div(home_slot[j], jnp.int32(OWN_SLOTS))
            which = lax.rem(home_slot[j], jnp.int32(OWN_SLOTS))
            slab = gathered[0]
            for o in range(1, tiles):
                slab = jnp.where(owner == o, gathered[o], slab)
            rows = slab[:levels]
            param = slab[OWN_SLOTS * levels : OWN_SLOTS * levels + 1]
            for i in range(1, OWN_SLOTS):
                rows = jnp.where(which == i, slab[i * levels : (i + 1) * levels], rows)
                at = OWN_SLOTS * levels + i
                param = jnp.where(which == i, slab[at : at + 1], param)
            rolled = [rows if d == 0 else pltpu.roll(rows, d * BY, 1) for d in range(segs)]
            _, x_half, _, seg = place[j]
            inside = (row_half == x_half) & (lane_seg == seg) & (home_on[j] > 0)
            for l in range(levels):
                laid = jnp.zeros((ROWS, LANES), jnp.float32)
                for d in range(segs):
                    spread = jnp.broadcast_to(rolled[d][l : l + 1, :], (ROWS, LANES))
                    pick = lax.rem(lane_seg - row_in + segs, segs) == d
                    laid = jnp.where(pick, spread, laid)
                weights_v[j, l] = jnp.where(inside, laid, 0.0)
            params.append([param[:, i : i + 1] for i in range(4)])
        return params

    def disk(src, params):
        found = [[[None] * levels for _ in range(2)] for _ in range(HOME_MOST)]
        for xt in range(x_tiles):
            rows = pl.ds(first + xt * ROWS, ROWS)
            for h in range(halves):
                on = [(place[j][0] == xt) & (place[j][2] == h) for j in range(HOME_MOST)]
                for c in range(2):
                    for l in range(levels):
                        cells = q[src, c, l, h, rows, :]
                        for j in range(HOME_MOST):
                            old = found[j][c][l]
                            found[j][c][l] = (
                                cells if old is None else jnp.where(on[j], cells, old)
                            )
        results = []
        for j in range(HOME_MOST):
            cosine, sine, coef, inverse = params[j]
            acc_u = jnp.zeros((ROWS, LANES), jnp.float32)
            acc_v = jnp.zeros((ROWS, LANES), jnp.float32)
            for l in range(levels):
                w = weights_v[j, l]
                acc_u += w * found[j][0][l]
                acc_v += w * found[j][1][l]
            normal = acc_u * cosine + acc_v * sine
            total = jnp.sum(jnp.sum(normal, axis=0, keepdims=True), axis=1, keepdims=True)
            speed = total * inverse
            pull = 0.5 * coef * jnp.abs(speed) * speed
            push = -TIME_STEP * pull
            results.append((push * cosine, push * sine, pull * speed))
        return results

    def add_force(dst, results):
        for xt in range(x_tiles):
            rows = pl.ds(first + xt * ROWS, ROWS)
            for h in range(halves):
                scale = []
                for j in range(HOME_MOST):
                    on = (place[j][0] == xt) & (place[j][2] == h)
                    scale.append([jnp.where(on, results[j][c], 0.0) for c in range(2)])
                for l in range(levels):
                    w = [weights_v[j, l] for j in range(HOME_MOST)]
                    for c in range(2):
                        force = scale[0][c] * w[0]
                        for j in range(1, HOME_MOST):
                            force += scale[j][c] * w[j]
                        q[dst, c, l, h, rows, :] += force

    def power_copy(d):
        return pltpu.make_async_remote_copy(
            src_ref=powers.at[tile],
            dst_ref=powers.at[tile],
            send_sem=power_send.at[d],
            recv_sem=power_recv.at[d],
            device_id=(layout, tile_at(d)),
            device_id_type=MESH,
        )

    power_row = jnp.zeros((1, LANES), jnp.float32)
    params = None
    for step in range(steps):
        src, dst = step % 2, (step + 1) % 2
        results = None
        if step > 0:
            results = disk(src, params)
        if step > 0 and step == steps - 1:
            for j in range(HOME_MOST):
                power_row = power_row + jnp.where(lane1 == j, results[j][2], 0.0)
            powers[tile] = power_row * (1.0 / steps)
            for d in range(1, tiles):
                power_copy(d).start()
        lax.fori_loop(
            1, x_tiles - 1, lambda xt, c: (stencil_tile(src, dst, xt), c)[1], 0
        )
        unpack_edge(step)
        lax.fori_loop(
            0,
            2,
            lambda i, c: (stencil_tile(src, dst, i * (x_tiles - 1)), c)[1],
            0,
        )
        if step == 0:
            for d in range(1, tiles):
                pltpu.make_async_remote_copy(
                    src_ref=gathered.at[tile],
                    dst_ref=gathered.at[tile_at(tiles - d)],
                    send_sem=gather_send.at[d],
                    recv_sem=gather_recv.at[d],
                    device_id=(layout, tile_at(d)),
                    device_id_type=MESH,
                ).wait_recv()
            params = lay_weights()
            results = disk(src, params)
        add_force(dst, results)
        if step < steps - 1:
            for j in range(HOME_MOST):
                power_row = power_row + jnp.where(lane1 == j, results[j][2], 0.0)
            pack_edge(step + 1, 0)
            pack_edge(step + 1, 1)
            send_edges(step + 1)

    final = steps % 2
    stores = [
        pltpu.make_async_copy(
            q.at[final, :, :, h, pl.ds(first, width_x), :],
            out_ref.at[0, :, :, :, pl.ds(h * LANES, LANES)],
            local_sem.at[3 + h],
        )
        for h in range(halves)
    ]
    for copy in stores:
        copy.start()

    for d in range(1, tiles):
        pltpu.make_async_remote_copy(
            src_ref=powers.at[tile],
            dst_ref=powers.at[tile_at(tiles - d)],
            send_sem=power_send.at[d],
            recv_sem=power_recv.at[d],
            device_id=(layout, tile_at(d)),
            device_id_type=MESH,
        ).wait_recv()
    lane_out = lax.broadcasted_iota(jnp.int32, (1, OWN_SLOTS), 1)
    answer = jnp.zeros((1, OWN_SLOTS), jnp.float32)
    rows_in = [powers[o] for o in range(tiles)]
    for j in range(OWN_SLOTS):
        home = lax.div(own_site[j], jnp.int32(HOME_MOST))
        which = lax.rem(own_site[j], jnp.int32(HOME_MOST))
        row = rows_in[0]
        for o in range(1, tiles):
            row = jnp.where(home == o, rows_in[o], row)
        value = jnp.sum(jnp.where(lane1 == which, row, 0.0), axis=1, keepdims=True)
        value = jnp.where(own_on[j] > 0, value, 0.0)
        answer = jnp.where(lane_out == j, value, answer)
    power_v[...] = answer
    last = pltpu.make_async_copy(power_v, power_ref, local_sem.at[0])
    last.start()

    for step in range(steps):
        @pl.when(tile > 0)
        def _():
            edge_copy(step, 0).wait_send()

        @pl.when(tile < tiles - 1)
        def _():
            edge_copy(step, 1).wait_send()

    @pl.when(tile == 0)
    def _():
        for d in range(1, layouts):
            plane_copy(d).wait_send()

    for d in range(1, tiles):
        gather_copy(d).wait_send()
        power_copy(d).wait_send()
    last.wait()
    for copy in stores:
        copy.wait()


def solution(mesh):
    tiles = mesh.shape["tile"]
    layouts = mesh.shape["layout"]

    def local(velocity, inflow, turbine_site, turbine_block, turbine_slot, smear, yaw, thrust_coef):
        _, _, levels, width_x, width_y = velocity.shape
        halves = width_y // LANES
        turbines = turbine_site.shape[1]
        edge_rows = 3 * levels * halves
        f32 = jnp.float32
        slab = -(-OWN_SLOTS * (levels + 1) // ROWS) * ROWS
        dma = pltpu.SemaphoreType.DMA
        anywhere = pl.BlockSpec(memory_space=pl.ANY)
        return pl.pallas_call(
            functools.partial(kernel, tiles, layouts, levels, width_x, halves, turbines),
            out_shape=(
                jax.ShapeDtypeStruct(velocity.shape, f32),
                jax.ShapeDtypeStruct(yaw.shape, f32),
            ),
            in_specs=[anywhere] * 8,
            out_specs=(anywhere, anywhere),
            scratch_shapes=[
                pltpu.VMEM((2, 3, levels, halves, width_x + 2 * ROWS, LANES), f32),
                pltpu.SMEM((1, turbines), jnp.int32),
                pltpu.SMEM((1, turbines), jnp.int32),
                pltpu.SMEM((1, turbines), jnp.int32),
                pltpu.VMEM(smear.shape[1:], f32),
                pltpu.VMEM(yaw.shape, f32),
                pltpu.VMEM(yaw.shape, f32),
                pltpu.VMEM((tiles, slab, LANES), f32),
                pltpu.VMEM((HOME_MOST, levels, ROWS, LANES), f32),
                pltpu.VMEM((layouts, 3, levels, width_y), f32),
                pltpu.VMEM((layouts, 2, edge_rows, LANES), f32),
                pltpu.VMEM((layouts, 2, edge_rows, LANES), f32),
                pltpu.VMEM((tiles, 1, LANES), f32),
                pltpu.VMEM((1, OWN_SLOTS), f32),
                dma((7 + halves,)),
                dma((tiles,)),
                dma((tiles,)),
                dma((layouts,)),
                dma((layouts,)),
                dma((layouts, 2)),
                dma((layouts, 2)),
                dma((tiles,)),
                dma((tiles,)),
            ],
            compiler_params=pltpu.CompilerParams(
                collective_id=0, has_side_effects=True, vmem_limit_bytes=24 * 1024 * 1024
            ),
        )(velocity, inflow, turbine_site, turbine_block, turbine_slot, smear, yaw, thrust_coef)

    in_specs = (
        P("layout", None, None, "tile", None),
        P("layout", None, None, None),
        P("layout", None),
        P("layout", None),
        P("layout", None),
        P("layout", "tile", None),
        P("layout", "tile"),
        P("layout", "tile"),
    )
    out_specs = (P("layout", None, None, "tile", None), P("layout", "tile"))
    return jax.shard_map(local, mesh=mesh, in_specs=in_specs, out_specs=out_specs, check_vma=False)
```

```python
import functools

import jax
import jax.numpy as jnp
from jax import lax
from jax.experimental import pallas as pl
from jax.experimental.pallas import tpu as pltpu
from jax.sharding import PartitionSpec as P

BX = 4
BY = 32
HOME_MOST = 3
OWN_SLOTS = 3
LANES = 128
ROWS = 8

TIME_STEP = 0.1
SMAG = 0.0256
FLOOR = 0.01

MESH = pl.DeviceIdType.MESH


def kernel(
    tiles, layouts, levels, width_x, halves, turbines,
    vel_ref, inflow_ref, site_ref, block_ref, slot_ref, smear_ref, yaw_ref, coef_ref,
    out_ref, power_ref,
    q, site_s, block_s, slot_s, smear_v, yaw_v, coef_v, gathered, weights_v,
    planes, edge_out, edge_in, powers,
    local_sem, gather_send, gather_recv, plane_send, plane_recv,
    edge_send, edge_recv, power_send, power_recv,
):
    tile = lax.axis_index("tile")
    layout = lax.axis_index("layout")
    steps = layouts
    fields = 3 * levels
    x_tiles = width_x // ROWS
    first = ROWS
    y_blocks = halves * LANES // BY
    segs = LANES // BY

    def tile_at(distance):
        return lax.rem(tile + distance, tiles)

    def layout_at(distance):
        return lax.rem(layout + distance, layouts)

    barrier = pltpu.get_barrier_semaphore()
    for d in range(1, tiles):
        pl.semaphore_signal(
            barrier, inc=1, device_id=(layout, tile_at(d)), device_id_type=MESH
        )
    for d in range(1, layouts):
        pl.semaphore_signal(
            barrier, inc=1, device_id=(layout_at(d), tile), device_id_type=MESH
        )

    loads = [
        pltpu.make_async_copy(smear_ref.at[:, 0], smear_v, local_sem.at[0]),
        pltpu.make_async_copy(yaw_ref, yaw_v, local_sem.at[1]),
        pltpu.make_async_copy(coef_ref, coef_v, local_sem.at[2]),
    ]
    field_loads = [
        pltpu.make_async_copy(
            vel_ref.at[0, :, :, :, pl.ds(h * LANES, LANES)],
            q.at[0, :, :, h, pl.ds(first, width_x), :],
            local_sem.at[3 + h],
        )
        for h in range(halves)
    ]
    base = 3 + halves
    plane_load = pltpu.make_async_copy(
        inflow_ref.at[0], planes.at[layout], local_sem.at[base]
    )
    list_loads = [
        pltpu.make_async_copy(site_ref, site_s, local_sem.at[base + 1]),
        pltpu.make_async_copy(block_ref, block_s, local_sem.at[base + 2]),
        pltpu.make_async_copy(slot_ref, slot_s, local_sem.at[base + 3]),
    ]
    for copy in loads + field_loads + [plane_load] + list_loads:
        copy.start()

    for copy in loads:
        copy.wait()
    lane1 = lax.broadcasted_iota(jnp.int32, (1, LANES), 1)
    for j in range(OWN_SLOTS):
        total = jnp.zeros((1, 1), jnp.float32)
        for l in range(levels):
            row = smear_v[pl.ds(j, 1), pl.ds(l * LANES, LANES)]
            gathered[tile, pl.ds(j * levels + l, 1), :] = row
            total = total + jnp.sum(row, axis=1, keepdims=True)
        angle = yaw_v[:, j : j + 1]
        packed = jnp.where(lane1 == 0, jnp.cos(angle), 0.0)
        packed = jnp.where(lane1 == 1, jnp.sin(angle), packed)
        packed = jnp.where(lane1 == 2, coef_v[:, j : j + 1], packed)
        packed = jnp.where(lane1 == 3, 1.0 / total, packed)
        gathered[tile, pl.ds(OWN_SLOTS * levels + j, 1), :] = packed

    for copy in field_loads:
        copy.wait()

    def pack_edge(step, side):
        row = first if side == 0 else first + width_x - 1
        for c in range(3):
            for l in range(levels):
                for h in range(halves):
                    i = (c * levels + l) * halves + h
                    edge_out[step, side, pl.ds(i, 1), :] = q[
                        step % 2, c, l, h, pl.ds(row, 1), :
                    ]

    def edge_copy(step, side):
        target = tile - 1 if side == 0 else tile + 1
        return pltpu.make_async_remote_copy(
            src_ref=edge_out.at[step, side],
            dst_ref=edge_in.at[step, 1 - side],
            send_sem=edge_send.at[step, side],
            recv_sem=edge_recv.at[step, 1 - side],
            device_id=(layout, target),
            device_id_type=MESH,
        )

    def send_edges(step):
        @pl.when(tile > 0)
        def _():
            edge_copy(step, 0).start()

        @pl.when(tile < tiles - 1)
        def _():
            edge_copy(step, 1).start()

    pack_edge(0, 0)
    pack_edge(0, 1)
    plane_load.wait()

    pl.semaphore_wait(barrier, tiles - 1 + layouts - 1)

    send_edges(0)

    def plane_copy(d):
        return pltpu.make_async_remote_copy(
            src_ref=planes.at[layout],
            dst_ref=planes.at[layout],
            send_sem=plane_send.at[d],
            recv_sem=plane_recv.at[d],
            device_id=(layout_at(d), tile),
            device_id_type=MESH,
        )

    @pl.when(tile == 0)
    def _():
        for d in range(1, layouts):
            plane_copy(d).start()

    def gather_copy(d):
        return pltpu.make_async_remote_copy(
            src_ref=gathered.at[tile],
            dst_ref=gathered.at[tile],
            send_sem=gather_send.at[d],
            recv_sem=gather_recv.at[d],
            device_id=(layout, tile_at(d)),
            device_id_type=MESH,
        )

    for d in range(1, tiles):
        gather_copy(d).start()

    for copy in list_loads:
        copy.wait()
    home_slot = [jnp.int32(0)] * HOME_MOST
    home_block = [jnp.int32(0)] * HOME_MOST
    home_on = [jnp.int32(0)] * HOME_MOST
    own_site = [jnp.int32(0)] * OWN_SLOTS
    own_on = [jnp.int32(0)] * OWN_SLOTS
    for k in range(turbines):
        site = site_s[0, k]
        block = block_s[0, k]
        slot = slot_s[0, k]
        for j in range(HOME_MOST):
            hit = site == tile * HOME_MOST + j
            home_slot[j] = jnp.where(hit, slot, home_slot[j])
            home_block[j] = jnp.where(hit, block, home_block[j])
            home_on[j] = jnp.where(hit, 1, home_on[j])
        for j in range(OWN_SLOTS):
            hit = slot == tile * OWN_SLOTS + j
            own_site[j] = jnp.where(hit, site, own_site[j])
            own_on[j] = jnp.where(hit, 1, own_on[j])

    lane = lax.broadcasted_iota(jnp.int32, (ROWS, LANES), 1)
    row_id = lax.broadcasted_iota(jnp.int32, (ROWS, LANES), 0)
    lane_seg = lane // BY
    row_in = row_id % BX
    row_half = row_id // BX

    def stencil_tile(src, put, xt):
        r = first + xt * ROWS
        here = pl.ds(r, ROWS)
        below_rows = pl.ds(r - 1, ROWS)
        above_rows = pl.ds(r + 1, ROWS)
        for l in range(levels):
            centre = [[q[src, c, l, h, here, :] for h in range(halves)] for c in range(3)]
            rolled_m = [
                [pltpu.roll(centre[c][h], 1, 1) for h in range(halves)] for c in range(3)
            ]
            rolled_p = [
                [pltpu.roll(centre[c][h], LANES - 1, 1) for h in range(halves)]
                for c in range(3)
            ]
            for h in range(halves):
                plus, minus = [], []
                for c in range(3):
                    mid = centre[c][h]
                    xm = q[src, c, l, h, below_rows, :]
                    xp = q[src, c, l, h, above_rows, :]
                    ym = jnp.where(lane == 0, rolled_m[c][h - 1], rolled_m[c][h])
                    yp = jnp.where(
                        lane == LANES - 1, rolled_p[c][(h + 1) % halves], rolled_p[c][h]
                    )
                    zm = mid if l == 0 else q[src, c, l - 1, h, here, :]
                    zp = mid if l == levels - 1 else q[src, c, l + 1, h, here, :]
                    plus.append([xp - mid, yp - mid, zp - mid])
                    minus.append([mid - xm, mid - ym, mid - zm])

                def grad(c, a):
                    return plus[c][a] + minus[c][a]

                gxx, gyy, gzz = grad(0, 0), grad(1, 1), grad(2, 2)
                sxy = grad(0, 1) + grad(1, 0)
                sxz = grad(0, 2) + grad(2, 0)
                syz = grad(1, 2) + grad(2, 1)
                strain = 2.0 * (gxx * gxx + gyy * gyy + gzz * gzz)
                strain = strain + sxy * sxy + sxz * sxz + syz * syz + 4.0 * FLOOR
                nu = (0.5 * SMAG * TIME_STEP) * (strain * lax.rsqrt(strain))
                ups, downs = [], []
                for a in range(3):
                    speed = TIME_STEP * centre[a][h]
                    ups.append(nu - jnp.minimum(speed, 0.0))
                    downs.append(nu + jnp.maximum(speed, 0.0))
                for c in range(3):
                    change = ups[0] * plus[c][0] - downs[0] * minus[c][0]
                    change += ups[1] * plus[c][1] - downs[1] * minus[c][1]
                    change += ups[2] * plus[c][2] - downs[2] * minus[c][2]
                    put(c, l, h, xt, centre[c][h] + change)

    def unpack_edge(step):
        src = step % 2
        left = pl.ds(first - 1, 1)
        right = pl.ds(first + width_x, 1)

        @pl.when(tile > 0)
        def _():
            edge_copy(step, 1).wait_recv()

        def fill(side, rows, value):
            for c in range(3):
                for l in range(levels):
                    for h in range(halves):
                        q[src, c, l, h, rows, :] = value(c, l, h)

        def received(side):
            return lambda c, l, h: edge_in[
                step, side, pl.ds((c * levels + l) * halves + h, 1), :
            ]

        @pl.when(tile > 0)
        def _():
            fill(0, left, received(0))

        @pl.when(tile == 0)
        def _():
            if step == 0:
                for d in range(1, layouts):
                    pltpu.make_async_remote_copy(
                        src_ref=planes.at[layout],
                        dst_ref=planes.at[layout_at(layouts - d)],
                        send_sem=plane_send.at[d],
                        recv_sem=plane_recv.at[d],
                        device_id=(layout_at(d), tile),
                        device_id_type=MESH,
                    ).wait_recv()
            fill(
                0,
                left,
                lambda c, l, h: planes[step, c, pl.ds(l, 1), pl.ds(h * LANES, LANES)],
            )

        @pl.when(tile < tiles - 1)
        def _():
            edge_copy(step, 0).wait_recv()
            fill(1, right, received(1))

        @pl.when(tile == tiles - 1)
        def _():
            fill(
                1,
                right,
                lambda c, l, h: q[src, c, l, h, pl.ds(first + width_x - 1, 1), :],
            )

    place = []
    for j in range(HOME_MOST):
        xb = lax.div(home_block[j], jnp.int32(y_blocks))
        yb = lax.rem(home_block[j], jnp.int32(y_blocks))
        per = ROWS // BX
        place.append(
            (
                lax.div(xb, jnp.int32(per)),
                lax.rem(xb, jnp.int32(per)),
                lax.div(yb, jnp.int32(segs)),
                lax.rem(yb, jnp.int32(segs)),
            )
        )

    def lay_weights():
        params = []
        for j in range(HOME_MOST):
            owner = lax.div(home_slot[j], jnp.int32(OWN_SLOTS))
            which = lax.rem(home_slot[j], jnp.int32(OWN_SLOTS))
            slab = gathered[0]
            for o in range(1, tiles):
                slab = jnp.where(owner == o, gathered[o], slab)
            rows = slab[:levels]
            param = slab[OWN_SLOTS * levels : OWN_SLOTS * levels + 1]
            for i in range(1, OWN_SLOTS):
                rows = jnp.where(which == i, slab[i * levels : (i + 1) * levels], rows)
                at = OWN_SLOTS * levels + i
                param = jnp.where(which == i, slab[at : at + 1], param)
            rolled = [rows if d == 0 else pltpu.roll(rows, d * BY, 1) for d in range(segs)]
            _, x_half, _, seg = place[j]
            inside = (row_half == x_half) & (lane_seg == seg) & (home_on[j] > 0)
            for l in range(levels):
                laid = jnp.zeros((ROWS, LANES), jnp.float32)
                for d in range(segs):
                    spread = jnp.broadcast_to(rolled[d][l : l + 1, :], (ROWS, LANES))
                    pick = lax.rem(lane_seg - row_in + segs, segs) == d
                    laid = jnp.where(pick, spread, laid)
                weights_v[j, l] = jnp.where(inside, laid, 0.0)
            params.append([param[:, i : i + 1] for i in range(4)])
        return params

    def disk(src, params):
        found = [[[None] * levels for _ in range(2)] for _ in range(HOME_MOST)]
        for xt in range(x_tiles):
            rows = pl.ds(first + xt * ROWS, ROWS)
            for h in range(halves):
                on = [(place[j][0] == xt) & (place[j][2] == h) for j in range(HOME_MOST)]
                for c in range(2):
                    for l in range(levels):
                        cells = q[src, c, l, h, rows, :]
                        for j in range(HOME_MOST):
                            old = found[j][c][l]
                            found[j][c][l] = (
                                cells if old is None else jnp.where(on[j], cells, old)
                            )
        results = []
        for j in range(HOME_MOST):
            cosine, sine, coef, inverse = params[j]
            acc_u = jnp.zeros((ROWS, LANES), jnp.float32)
            acc_v = jnp.zeros((ROWS, LANES), jnp.float32)
            for l in range(levels):
                w = weights_v[j, l]
                acc_u += w * found[j][0][l]
                acc_v += w * found[j][1][l]
            normal = acc_u * cosine + acc_v * sine
            total = jnp.sum(jnp.sum(normal, axis=0, keepdims=True), axis=1, keepdims=True)
            speed = total * inverse
            pull = 0.5 * coef * jnp.abs(speed) * speed
            push = -TIME_STEP * pull
            results.append((push * cosine, push * sine, pull * speed))
        return results

    def add_force(get, put, results):
        for xt in range(x_tiles):
            for h in range(halves):
                scale = []
                for j in range(HOME_MOST):
                    on = (place[j][0] == xt) & (place[j][2] == h)
                    scale.append([jnp.where(on, results[j][c], 0.0) for c in range(2)])
                for l in range(levels):
                    w = [weights_v[j, l] for j in range(HOME_MOST)]
                    for c in range(2):
                        force = scale[0][c] * w[0]
                        for j in range(1, HOME_MOST):
                            force += scale[j][c] * w[j]
                        put(c, l, h, xt, get(c, l, h, xt) + force)

    def power_copy(d):
        return pltpu.make_async_remote_copy(
            src_ref=powers.at[tile],
            dst_ref=powers.at[tile],
            send_sem=power_send.at[d],
            recv_sem=power_recv.at[d],
            device_id=(layout, tile_at(d)),
            device_id_type=MESH,
        )

    def access(step):
        dst = (step + 1) % 2

        def where_at(c, l, h, xt):
            if step == steps - 1:
                return out_ref, (0, c, l, pl.ds(xt * ROWS, ROWS), pl.ds(h * LANES, LANES))
            return q, (dst, c, l, h, pl.ds(first + xt * ROWS, ROWS), slice(None))

        def get(*at):
            ref, index = where_at(*at)
            return ref[index]

        def put(c, l, h, xt, value):
            ref, index = where_at(c, l, h, xt)
            ref[index] = value

        return get, put

    power_row = jnp.zeros((1, LANES), jnp.float32)
    params = None
    for step in range(steps):
        src, dst = step % 2, (step + 1) % 2
        get, put = access(step)
        results = None
        if step > 0:
            results = disk(src, params)
        if step > 0 and step == steps - 1:
            for j in range(HOME_MOST):
                power_row = power_row + jnp.where(lane1 == j, results[j][2], 0.0)
            powers[tile] = power_row * (1.0 / steps)
            for d in range(1, tiles):
                power_copy(d).start()
        lax.fori_loop(
            1, x_tiles - 1, lambda xt, c: (stencil_tile(src, put, xt), c)[1], 0
        )
        unpack_edge(step)
        lax.fori_loop(
            0,
            2,
            lambda i, c: (stencil_tile(src, put, i * (x_tiles - 1)), c)[1],
            0,
        )
        if step == 0:
            for d in range(1, tiles):
                pltpu.make_async_remote_copy(
                    src_ref=gathered.at[tile],
                    dst_ref=gathered.at[tile_at(tiles - d)],
                    send_sem=gather_send.at[d],
                    recv_sem=gather_recv.at[d],
                    device_id=(layout, tile_at(d)),
                    device_id_type=MESH,
                ).wait_recv()
            params = lay_weights()
            results = disk(src, params)
        add_force(get, put, results)
        if step < steps - 1:
            for j in range(HOME_MOST):
                power_row = power_row + jnp.where(lane1 == j, results[j][2], 0.0)
            pack_edge(step + 1, 0)
            pack_edge(step + 1, 1)
            send_edges(step + 1)

    for d in range(1, tiles):
        pltpu.make_async_remote_copy(
            src_ref=powers.at[tile],
            dst_ref=powers.at[tile_at(tiles - d)],
            send_sem=power_send.at[d],
            recv_sem=power_recv.at[d],
            device_id=(layout, tile_at(d)),
            device_id_type=MESH,
        ).wait_recv()
    lane_out = lax.broadcasted_iota(jnp.int32, (1, OWN_SLOTS), 1)
    answer = jnp.zeros((1, OWN_SLOTS), jnp.float32)
    rows_in = [powers[o] for o in range(tiles)]
    for j in range(OWN_SLOTS):
        home = lax.div(own_site[j], jnp.int32(HOME_MOST))
        which = lax.rem(own_site[j], jnp.int32(HOME_MOST))
        row = rows_in[0]
        for o in range(1, tiles):
            row = jnp.where(home == o, rows_in[o], row)
        value = jnp.sum(jnp.where(lane1 == which, row, 0.0), axis=1, keepdims=True)
        value = jnp.where(own_on[j] > 0, value, 0.0)
        answer = jnp.where(lane_out == j, value, answer)
    power_ref[...] = answer

    for step in range(steps):
        @pl.when(tile > 0)
        def _():
            edge_copy(step, 0).wait_send()

        @pl.when(tile < tiles - 1)
        def _():
            edge_copy(step, 1).wait_send()

    @pl.when(tile == 0)
    def _():
        for d in range(1, layouts):
            plane_copy(d).wait_send()

    for d in range(1, tiles):
        gather_copy(d).wait_send()
        power_copy(d).wait_send()


def solution(mesh):
    tiles = mesh.shape["tile"]
    layouts = mesh.shape["layout"]

    def local(velocity, inflow, turbine_site, turbine_block, turbine_slot, smear, yaw, thrust_coef):
        _, _, levels, width_x, width_y = velocity.shape
        halves = width_y // LANES
        turbines = turbine_site.shape[1]
        edge_rows = 3 * levels * halves
        f32 = jnp.float32
        slab = -(-OWN_SLOTS * (levels + 1) // ROWS) * ROWS
        dma = pltpu.SemaphoreType.DMA
        inside = pl.BlockSpec(memory_space=pltpu.VMEM)
        return pl.pallas_call(
            functools.partial(kernel, tiles, layouts, levels, width_x, halves, turbines),
            out_shape=(
                pltpu.VMEM(velocity.shape, f32),
                pltpu.VMEM(yaw.shape, f32),
            ),
            in_specs=[pl.BlockSpec(memory_space=pltpu.HBM)] * 8,
            out_specs=(inside, inside),
            scratch_shapes=[
                pltpu.VMEM((2, 3, levels, halves, width_x + 2 * ROWS, LANES), f32),
                pltpu.SMEM((1, turbines), jnp.int32),
                pltpu.SMEM((1, turbines), jnp.int32),
                pltpu.SMEM((1, turbines), jnp.int32),
                pltpu.VMEM(smear.shape[1:], f32),
                pltpu.VMEM(yaw.shape, f32),
                pltpu.VMEM(yaw.shape, f32),
                pltpu.VMEM((tiles, slab, LANES), f32),
                pltpu.VMEM((HOME_MOST, levels, ROWS, LANES), f32),
                pltpu.VMEM((layouts, 3, levels, width_y), f32),
                pltpu.VMEM((layouts, 2, edge_rows, LANES), f32),
                pltpu.VMEM((layouts, 2, edge_rows, LANES), f32),
                pltpu.VMEM((tiles, 1, LANES), f32),
                dma((7 + halves,)),
                dma((tiles,)),
                dma((tiles,)),
                dma((layouts,)),
                dma((layouts,)),
                dma((layouts, 2)),
                dma((layouts, 2)),
                dma((tiles,)),
                dma((tiles,)),
            ],
            compiler_params=pltpu.CompilerParams(
                collective_id=0, has_side_effects=True, vmem_limit_bytes=24 * 1024 * 1024
            ),
        )(
            velocity, inflow, turbine_site, turbine_block, turbine_slot,
            jnp.transpose(smear, (1, 0, 2)), yaw, thrust_coef,
        )

    in_specs = (
        P("layout", None, None, "tile", None),
        P("layout", None, None, None),
        P("layout", None),
        P("layout", None),
        P("layout", None),
        P("layout", "tile", None),
        P("layout", "tile"),
        P("layout", "tile"),
    )
    out_specs = (P("layout", None, None, "tile", None), P("layout", "tile"))
    return jax.shard_map(local, mesh=mesh, in_specs=in_specs, out_specs=out_specs, check_vma=False)
```

```python
import functools

import jax
import jax.numpy as jnp
from jax import lax
from jax.experimental import pallas as pl
from jax.experimental.pallas import tpu as pltpu
from jax.sharding import PartitionSpec as P

BX = 4
BY = 32
HOME_MOST = 3
OWN_SLOTS = 3
LANES = 128
ROWS = 8

TIME_STEP = 0.1
SMAG = 0.0256
FLOOR = 0.01

MESH = pl.DeviceIdType.MESH


def kernel(
    tiles, layouts, levels, width_x, halves, turbines,
    vel_ref, inflow_ref, site_ref, block_ref, slot_ref, smear_ref, yaw_ref, coef_ref,
    out_ref, power_ref,
    q, site_s, block_s, slot_s, smear_v, yaw_v, coef_v, gathered, weights_v,
    planes, edge_out, edge_in, powers,
    local_sem, gather_send, gather_recv, plane_send, plane_recv,
    edge_send, edge_recv, power_send, power_recv,
):
    tile = lax.axis_index("tile")
    layout = lax.axis_index("layout")
    steps = layouts
    fields = 3 * levels
    x_tiles = width_x // ROWS
    first = ROWS
    y_blocks = halves * LANES // BY
    segs = LANES // BY

    def tile_at(distance):
        return lax.rem(tile + distance, tiles)

    def layout_at(distance):
        return lax.rem(layout + distance, layouts)

    barrier = pltpu.get_barrier_semaphore()
    for d in range(1, tiles):
        pl.semaphore_signal(
            barrier, inc=1, device_id=(layout, tile_at(d)), device_id_type=MESH
        )
    for d in range(1, layouts):
        pl.semaphore_signal(
            barrier, inc=1, device_id=(layout_at(d), tile), device_id_type=MESH
        )

    loads = [
        pltpu.make_async_copy(smear_ref.at[:, 0], smear_v, local_sem.at[0]),
        pltpu.make_async_copy(yaw_ref, yaw_v, local_sem.at[1]),
        pltpu.make_async_copy(coef_ref, coef_v, local_sem.at[2]),
    ]
    field_loads = [
        pltpu.make_async_copy(
            vel_ref.at[0, :, :, :, pl.ds(h * LANES, LANES)],
            q.at[0, :, :, h, pl.ds(first, width_x), :],
            local_sem.at[3 + h],
        )
        for h in range(halves)
    ]
    base = 3 + halves
    plane_load = pltpu.make_async_copy(
        inflow_ref.at[0], planes.at[layout], local_sem.at[base]
    )
    list_loads = [
        pltpu.make_async_copy(site_ref, site_s, local_sem.at[base + 1]),
        pltpu.make_async_copy(block_ref, block_s, local_sem.at[base + 2]),
        pltpu.make_async_copy(slot_ref, slot_s, local_sem.at[base + 3]),
    ]
    for copy in loads + field_loads + [plane_load] + list_loads:
        copy.start()

    for copy in loads:
        copy.wait()
    lane1 = lax.broadcasted_iota(jnp.int32, (1, LANES), 1)
    for j in range(OWN_SLOTS):
        total = jnp.zeros((1, 1), jnp.float32)
        for l in range(levels):
            row = smear_v[pl.ds(j, 1), pl.ds(l * LANES, LANES)]
            gathered[tile, pl.ds(j * levels + l, 1), :] = row
            total = total + jnp.sum(row, axis=1, keepdims=True)
        angle = yaw_v[:, j : j + 1]
        packed = jnp.where(lane1 == 0, jnp.cos(angle), 0.0)
        packed = jnp.where(lane1 == 1, jnp.sin(angle), packed)
        packed = jnp.where(lane1 == 2, coef_v[:, j : j + 1], packed)
        packed = jnp.where(lane1 == 3, 1.0 / total, packed)
        gathered[tile, pl.ds(OWN_SLOTS * levels + j, 1), :] = packed

    for copy in field_loads:
        copy.wait()

    def pack_edge(step, side):
        row = first if side == 0 else first + width_x - 1
        for c in range(3):
            for l in range(levels):
                for h in range(halves):
                    i = (c * levels + l) * halves + h
                    edge_out[step, side, pl.ds(i, 1), :] = q[
                        step % 2, c, l, h, pl.ds(row, 1), :
                    ]

    def edge_copy(step, side):
        target = tile - 1 if side == 0 else tile + 1
        return pltpu.make_async_remote_copy(
            src_ref=edge_out.at[step, side],
            dst_ref=edge_in.at[step, 1 - side],
            send_sem=edge_send.at[step, side],
            recv_sem=edge_recv.at[step, 1 - side],
            device_id=(layout, target),
            device_id_type=MESH,
        )

    def send_edges(step):
        @pl.when(tile > 0)
        def _():
            edge_copy(step, 0).start()

        @pl.when(tile < tiles - 1)
        def _():
            edge_copy(step, 1).start()

    pack_edge(0, 0)
    pack_edge(0, 1)
    plane_load.wait()

    pl.semaphore_wait(barrier, tiles - 1 + layouts - 1)

    send_edges(0)

    def plane_copy(d):
        return pltpu.make_async_remote_copy(
            src_ref=planes.at[layout],
            dst_ref=planes.at[layout],
            send_sem=plane_send.at[d],
            recv_sem=plane_recv.at[d],
            device_id=(layout_at(d), tile),
            device_id_type=MESH,
        )

    @pl.when(tile == 0)
    def _():
        for d in range(1, layouts):
            plane_copy(d).start()

    def gather_copy(d):
        return pltpu.make_async_remote_copy(
            src_ref=gathered.at[tile],
            dst_ref=gathered.at[tile],
            send_sem=gather_send.at[d],
            recv_sem=gather_recv.at[d],
            device_id=(layout, tile_at(d)),
            device_id_type=MESH,
        )

    for d in range(1, tiles):
        gather_copy(d).start()

    for copy in list_loads:
        copy.wait()
    home_slot = [jnp.int32(0)] * HOME_MOST
    home_block = [jnp.int32(0)] * HOME_MOST
    home_on = [jnp.int32(0)] * HOME_MOST
    own_site = [jnp.int32(0)] * OWN_SLOTS
    own_on = [jnp.int32(0)] * OWN_SLOTS
    for k in range(turbines):
        site = site_s[0, k]
        block = block_s[0, k]
        slot = slot_s[0, k]
        for j in range(HOME_MOST):
            hit = site == tile * HOME_MOST + j
            home_slot[j] = jnp.where(hit, slot, home_slot[j])
            home_block[j] = jnp.where(hit, block, home_block[j])
            home_on[j] = jnp.where(hit, 1, home_on[j])
        for j in range(OWN_SLOTS):
            hit = slot == tile * OWN_SLOTS + j
            own_site[j] = jnp.where(hit, site, own_site[j])
            own_on[j] = jnp.where(hit, 1, own_on[j])

    lane = lax.broadcasted_iota(jnp.int32, (ROWS, LANES), 1)
    row_id = lax.broadcasted_iota(jnp.int32, (ROWS, LANES), 0)
    lane_seg = lane // BY
    row_in = row_id % BX
    row_half = row_id // BX

    def stencil_tile(src, put, xt):
        r = first + xt * ROWS
        here = pl.ds(r, ROWS)
        below_rows = pl.ds(r - 1, ROWS)
        above_rows = pl.ds(r + 1, ROWS)
        for l in range(levels):
            centre = [[q[src, c, l, h, here, :] for h in range(halves)] for c in range(3)]
            rolled_m = [
                [pltpu.roll(centre[c][h], 1, 1) for h in range(halves)] for c in range(3)
            ]
            rolled_p = [
                [pltpu.roll(centre[c][h], LANES - 1, 1) for h in range(halves)]
                for c in range(3)
            ]
            for h in range(halves):
                plus, minus = [], []
                for c in range(3):
                    mid = centre[c][h]
                    xm = q[src, c, l, h, below_rows, :]
                    xp = q[src, c, l, h, above_rows, :]
                    ym = jnp.where(lane == 0, rolled_m[c][h - 1], rolled_m[c][h])
                    yp = jnp.where(
                        lane == LANES - 1, rolled_p[c][(h + 1) % halves], rolled_p[c][h]
                    )
                    zm = mid if l == 0 else q[src, c, l - 1, h, here, :]
                    zp = mid if l == levels - 1 else q[src, c, l + 1, h, here, :]
                    plus.append([xp - mid, yp - mid, zp - mid])
                    minus.append([mid - xm, mid - ym, mid - zm])

                def grad(c, a):
                    return plus[c][a] + minus[c][a]

                gxx, gyy, gzz = grad(0, 0), grad(1, 1), grad(2, 2)
                sxy = grad(0, 1) + grad(1, 0)
                sxz = grad(0, 2) + grad(2, 0)
                syz = grad(1, 2) + grad(2, 1)
                strain = 2.0 * (gxx * gxx + gyy * gyy + gzz * gzz)
                strain = strain + sxy * sxy + sxz * sxz + syz * syz + 4.0 * FLOOR
                nu = (0.5 * SMAG * TIME_STEP) * (strain * lax.rsqrt(strain))
                ups, downs = [], []
                for a in range(3):
                    speed = TIME_STEP * centre[a][h]
                    ups.append(nu - jnp.minimum(speed, 0.0))
                    downs.append(nu + jnp.maximum(speed, 0.0))
                for c in range(3):
                    change = ups[0] * plus[c][0] - downs[0] * minus[c][0]
                    change += ups[1] * plus[c][1] - downs[1] * minus[c][1]
                    change += ups[2] * plus[c][2] - downs[2] * minus[c][2]
                    put(c, l, h, xt, centre[c][h] + change)

    def unpack_edge(step):
        src = step % 2
        left = pl.ds(first - 1, 1)
        right = pl.ds(first + width_x, 1)

        @pl.when(tile > 0)
        def _():
            edge_copy(step, 1).wait_recv()

        def fill(side, rows, value):
            for c in range(3):
                for l in range(levels):
                    for h in range(halves):
                        q[src, c, l, h, rows, :] = value(c, l, h)

        def received(side):
            return lambda c, l, h: edge_in[
                step, side, pl.ds((c * levels + l) * halves + h, 1), :
            ]

        @pl.when(tile > 0)
        def _():
            fill(0, left, received(0))

        @pl.when(tile == 0)
        def _():
            if step == 0:
                for d in range(1, layouts):
                    pltpu.make_async_remote_copy(
                        src_ref=planes.at[layout],
                        dst_ref=planes.at[layout_at(layouts - d)],
                        send_sem=plane_send.at[d],
                        recv_sem=plane_recv.at[d],
                        device_id=(layout_at(d), tile),
                        device_id_type=MESH,
                    ).wait_recv()
            fill(
                0,
                left,
                lambda c, l, h: planes[step, c, pl.ds(l, 1), pl.ds(h * LANES, LANES)],
            )

        @pl.when(tile < tiles - 1)
        def _():
            edge_copy(step, 0).wait_recv()
            fill(1, right, received(1))

        @pl.when(tile == tiles - 1)
        def _():
            fill(
                1,
                right,
                lambda c, l, h: q[src, c, l, h, pl.ds(first + width_x - 1, 1), :],
            )

    place = []
    for j in range(HOME_MOST):
        xb = lax.div(home_block[j], jnp.int32(y_blocks))
        yb = lax.rem(home_block[j], jnp.int32(y_blocks))
        per = ROWS // BX
        place.append(
            (
                lax.div(xb, jnp.int32(per)),
                lax.rem(xb, jnp.int32(per)),
                lax.div(yb, jnp.int32(segs)),
                lax.rem(yb, jnp.int32(segs)),
            )
        )

    def lay_weights():
        params = []
        for j in range(HOME_MOST):
            owner = lax.div(home_slot[j], jnp.int32(OWN_SLOTS))
            which = lax.rem(home_slot[j], jnp.int32(OWN_SLOTS))
            slab = gathered[0]
            for o in range(1, tiles):
                slab = jnp.where(owner == o, gathered[o], slab)
            rows = slab[:levels]
            param = slab[OWN_SLOTS * levels : OWN_SLOTS * levels + 1]
            for i in range(1, OWN_SLOTS):
                rows = jnp.where(which == i, slab[i * levels : (i + 1) * levels], rows)
                at = OWN_SLOTS * levels + i
                param = jnp.where(which == i, slab[at : at + 1], param)
            rolled = [rows if d == 0 else pltpu.roll(rows, d * BY, 1) for d in range(segs)]
            _, x_half, _, seg = place[j]
            inside = (row_half == x_half) & (lane_seg == seg) & (home_on[j] > 0)
            for l in range(levels):
                laid = jnp.zeros((ROWS, LANES), jnp.float32)
                for d in range(segs):
                    spread = jnp.broadcast_to(rolled[d][l : l + 1, :], (ROWS, LANES))
                    pick = lax.rem(lane_seg - row_in + segs, segs) == d
                    laid = jnp.where(pick, spread, laid)
                weights_v[j, l] = jnp.where(inside, laid, 0.0)
            params.append([param[:, i : i + 1] for i in range(4)])
        return params

    def disk(src, params):
        found = [[[None] * levels for _ in range(2)] for _ in range(HOME_MOST)]
        for xt in range(x_tiles):
            rows = pl.ds(first + xt * ROWS, ROWS)
            for h in range(halves):
                on = [(place[j][0] == xt) & (place[j][2] == h) for j in range(HOME_MOST)]
                for c in range(2):
                    for l in range(levels):
                        cells = q[src, c, l, h, rows, :]
                        for j in range(HOME_MOST):
                            old = found[j][c][l]
                            found[j][c][l] = (
                                cells if old is None else jnp.where(on[j], cells, old)
                            )
        results = []
        for j in range(HOME_MOST):
            cosine, sine, coef, inverse = params[j]
            acc_u = jnp.zeros((ROWS, LANES), jnp.float32)
            acc_v = jnp.zeros((ROWS, LANES), jnp.float32)
            for l in range(levels):
                w = weights_v[j, l]
                acc_u += w * found[j][0][l]
                acc_v += w * found[j][1][l]
            normal = acc_u * cosine + acc_v * sine
            total = jnp.sum(jnp.sum(normal, axis=0, keepdims=True), axis=1, keepdims=True)
            speed = total * inverse
            pull = 0.5 * coef * jnp.abs(speed) * speed
            push = -TIME_STEP * pull
            results.append((push * cosine, push * sine, pull * speed))
        return results

    def add_force(get, put, results):
        for xt in range(x_tiles):
            for h in range(halves):
                scale = []
                for j in range(HOME_MOST):
                    on = (place[j][0] == xt) & (place[j][2] == h)
                    scale.append([jnp.where(on, results[j][c], 0.0) for c in range(2)])
                for l in range(levels):
                    w = [weights_v[j, l] for j in range(HOME_MOST)]
                    for c in range(2):
                        force = scale[0][c] * w[0]
                        for j in range(1, HOME_MOST):
                            force += scale[j][c] * w[j]
                        put(c, l, h, xt, get(c, l, h, xt) + force)

    def power_copy(d):
        return pltpu.make_async_remote_copy(
            src_ref=powers.at[tile],
            dst_ref=powers.at[tile],
            send_sem=power_send.at[d],
            recv_sem=power_recv.at[d],
            device_id=(layout, tile_at(d)),
            device_id_type=MESH,
        )

    def access(step):
        dst = (step + 1) % 2

        def where_at(c, l, h, xt):
            if step == steps - 1:
                return out_ref, (0, c, l, pl.ds(xt * ROWS, ROWS), pl.ds(h * LANES, LANES))
            return q, (dst, c, l, h, pl.ds(first + xt * ROWS, ROWS), slice(None))

        def get(*at):
            ref, index = where_at(*at)
            return ref[index]

        def put(c, l, h, xt, value):
            ref, index = where_at(c, l, h, xt)
            ref[index] = value

        return get, put

    power_row = jnp.zeros((1, LANES), jnp.float32)
    params = None
    for step in range(steps):
        src, dst = step % 2, (step + 1) % 2
        get, put = access(step)
        results = None
        if step > 0:
            results = disk(src, params)
        if step > 0 and step == steps - 1:
            for j in range(HOME_MOST):
                power_row = power_row + jnp.where(lane1 == j, results[j][2], 0.0)
            powers[tile] = power_row * (1.0 / steps)
            for d in range(1, tiles):
                power_copy(d).start()
        lax.fori_loop(
            1, x_tiles - 1, lambda xt, c: (stencil_tile(src, put, xt), c)[1], 0
        )
        unpack_edge(step)
        lax.fori_loop(
            0,
            2,
            lambda i, c: (stencil_tile(src, put, i * (x_tiles - 1)), c)[1],
            0,
        )
        if step == 0:
            for d in range(1, tiles):
                pltpu.make_async_remote_copy(
                    src_ref=gathered.at[tile],
                    dst_ref=gathered.at[tile_at(tiles - d)],
                    send_sem=gather_send.at[d],
                    recv_sem=gather_recv.at[d],
                    device_id=(layout, tile_at(d)),
                    device_id_type=MESH,
                ).wait_recv()
            params = lay_weights()
            results = disk(src, params)
        add_force(get, put, results)
        if step < steps - 1:
            for j in range(HOME_MOST):
                power_row = power_row + jnp.where(lane1 == j, results[j][2], 0.0)
            pack_edge(step + 1, 0)
            pack_edge(step + 1, 1)
            send_edges(step + 1)

    for d in range(1, tiles):
        pltpu.make_async_remote_copy(
            src_ref=powers.at[tile],
            dst_ref=powers.at[tile_at(tiles - d)],
            send_sem=power_send.at[d],
            recv_sem=power_recv.at[d],
            device_id=(layout, tile_at(d)),
            device_id_type=MESH,
        ).wait_recv()
    lane_out = lax.broadcasted_iota(jnp.int32, (1, OWN_SLOTS), 1)
    answer = jnp.zeros((1, OWN_SLOTS), jnp.float32)
    rows_in = [powers[o] for o in range(tiles)]
    for j in range(OWN_SLOTS):
        home = lax.div(own_site[j], jnp.int32(HOME_MOST))
        which = lax.rem(own_site[j], jnp.int32(HOME_MOST))
        row = rows_in[0]
        for o in range(1, tiles):
            row = jnp.where(home == o, rows_in[o], row)
        value = jnp.sum(jnp.where(lane1 == which, row, 0.0), axis=1, keepdims=True)
        value = jnp.where(own_on[j] > 0, value, 0.0)
        answer = jnp.where(lane_out == j, value, answer)
    power_ref[...] = answer

    for step in range(steps):
        @pl.when(tile > 0)
        def _():
            edge_copy(step, 0).wait_send()

        @pl.when(tile < tiles - 1)
        def _():
            edge_copy(step, 1).wait_send()

    @pl.when(tile == 0)
    def _():
        for d in range(1, layouts):
            plane_copy(d).wait_send()

    for d in range(1, tiles):
        gather_copy(d).wait_send()
        power_copy(d).wait_send()


def solution(mesh):
    tiles = mesh.shape["tile"]
    layouts = mesh.shape["layout"]

    def local(velocity, inflow, turbine_site, turbine_block, turbine_slot, smear, yaw, thrust_coef):
        _, _, levels, width_x, width_y = velocity.shape
        halves = width_y // LANES
        turbines = turbine_site.shape[1]
        edge_rows = 3 * levels * halves
        f32 = jnp.float32
        slab = -(-OWN_SLOTS * (levels + 1) // ROWS) * ROWS
        dma = pltpu.SemaphoreType.DMA
        inside = pl.BlockSpec(memory_space=pltpu.VMEM)
        return pl.pallas_call(
            functools.partial(kernel, tiles, layouts, levels, width_x, halves, turbines),
            out_shape=(
                pltpu.VMEM(velocity.shape, f32),
                pltpu.VMEM(yaw.shape, f32),
            ),
            in_specs=[pl.BlockSpec(memory_space=pltpu.HBM)] * 8,
            out_specs=(inside, inside),
            scratch_shapes=[
                pltpu.VMEM((2, 3, levels, halves, width_x + 2 * ROWS, LANES), f32),
                pltpu.SMEM((1, turbines), jnp.int32),
                pltpu.SMEM((1, turbines), jnp.int32),
                pltpu.SMEM((1, turbines), jnp.int32),
                pltpu.VMEM(smear.shape[1:], f32),
                pltpu.VMEM(yaw.shape, f32),
                pltpu.VMEM(yaw.shape, f32),
                pltpu.VMEM((tiles, slab, LANES), f32),
                pltpu.VMEM((HOME_MOST, levels, ROWS, LANES), f32),
                pltpu.VMEM((layouts, 3, levels, width_y), f32),
                pltpu.VMEM((layouts, 2, edge_rows, LANES), f32),
                pltpu.VMEM((layouts, 2, edge_rows, LANES), f32),
                pltpu.VMEM((tiles, 1, LANES), f32),
                dma((7 + halves,)),
                dma((tiles,)),
                dma((tiles,)),
                dma((layouts,)),
                dma((layouts,)),
                dma((layouts, 2)),
                dma((layouts, 2)),
                dma((tiles,)),
                dma((tiles,)),
            ],
            compiler_params=pltpu.CompilerParams(
                collective_id=0, has_side_effects=True, vmem_limit_bytes=60 * 1024 * 1024
            ),
        )(
            velocity, inflow, turbine_site, turbine_block, turbine_slot,
            jnp.transpose(smear, (1, 0, 2)), yaw, thrust_coef,
        )

    in_specs = (
        P("layout", None, None, "tile", None),
        P("layout", None, None, None),
        P("layout", None),
        P("layout", None),
        P("layout", None),
        P("layout", "tile", None),
        P("layout", "tile"),
        P("layout", "tile"),
    )
    out_specs = (P("layout", None, None, "tile", None), P("layout", "tile"))
    return jax.shard_map(local, mesh=mesh, in_specs=in_specs, out_specs=out_specs, check_vma=False)
```

```python
import functools

import jax
import jax.numpy as jnp
from jax import lax
from jax.experimental import pallas as pl
from jax.experimental.pallas import tpu as pltpu
from jax.sharding import PartitionSpec as P

BX = 4
BY = 32
HOME_MOST = 3
OWN_SLOTS = 3
LANES = 128
ROWS = 8

TIME_STEP = 0.1
SMAG = 0.0256
FLOOR = 0.01

MESH = pl.DeviceIdType.MESH


def kernel(
    tiles, layouts, levels, width_x, halves, turbines,
    vel_ref, inflow_ref, site_ref, block_ref, slot_ref, smear_ref, yaw_ref, coef_ref,
    out_ref, power_ref,
    q, site_s, block_s, slot_s, smear_v, yaw_v, coef_v, gathered, weights_v,
    planes, edge_out, edge_in, powers,
    local_sem, gather_send, gather_recv, plane_send, plane_recv,
    edge_send, edge_recv, power_send, power_recv,
):
    tile = lax.axis_index("tile")
    layout = lax.axis_index("layout")
    steps = layouts
    fields = 3 * levels
    x_tiles = width_x // ROWS
    first = ROWS
    y_blocks = halves * LANES // BY
    segs = LANES // BY

    def tile_at(distance):
        return lax.rem(tile + distance, tiles)

    def layout_at(distance):
        return lax.rem(layout + distance, layouts)

    barrier = pltpu.get_barrier_semaphore()
    for d in range(1, tiles):
        pl.semaphore_signal(
            barrier, inc=1, device_id=(layout, tile_at(d)), device_id_type=MESH
        )
    for d in range(1, layouts):
        pl.semaphore_signal(
            barrier, inc=1, device_id=(layout_at(d), tile), device_id_type=MESH
        )

    loads = [
        pltpu.make_async_copy(smear_ref.at[:, 0], smear_v, local_sem.at[0]),
        pltpu.make_async_copy(yaw_ref, yaw_v, local_sem.at[1]),
        pltpu.make_async_copy(coef_ref, coef_v, local_sem.at[2]),
    ]
    field_loads = [
        pltpu.make_async_copy(
            vel_ref.at[0, :, :, :, pl.ds(h * LANES, LANES)],
            q.at[0, :, :, h, pl.ds(first, width_x), :],
            local_sem.at[3 + h],
        )
        for h in range(halves)
    ]
    base = 3 + halves
    plane_load = pltpu.make_async_copy(
        inflow_ref.at[0], planes.at[layout], local_sem.at[base]
    )
    list_loads = [
        pltpu.make_async_copy(site_ref, site_s, local_sem.at[base + 1]),
        pltpu.make_async_copy(block_ref, block_s, local_sem.at[base + 2]),
        pltpu.make_async_copy(slot_ref, slot_s, local_sem.at[base + 3]),
    ]
    for copy in loads + field_loads + [plane_load] + list_loads:
        copy.start()

    for copy in loads:
        copy.wait()
    lane1 = lax.broadcasted_iota(jnp.int32, (1, LANES), 1)
    for j in range(OWN_SLOTS):
        total = jnp.zeros((1, 1), jnp.float32)
        for l in range(levels):
            row = smear_v[pl.ds(j, 1), pl.ds(l * LANES, LANES)]
            gathered[tile, pl.ds(j * levels + l, 1), :] = row
            total = total + jnp.sum(row, axis=1, keepdims=True)
        angle = yaw_v[:, j : j + 1]
        packed = jnp.where(lane1 == 0, jnp.cos(angle), 0.0)
        packed = jnp.where(lane1 == 1, jnp.sin(angle), packed)
        packed = jnp.where(lane1 == 2, coef_v[:, j : j + 1], packed)
        packed = jnp.where(lane1 == 3, 1.0 / total, packed)
        gathered[tile, pl.ds(OWN_SLOTS * levels + j, 1), :] = packed

    def pack_edge(step, side):
        row = first if side == 0 else first + width_x - 1
        for c in range(3):
            for l in range(levels):
                for h in range(halves):
                    i = (c * levels + l) * halves + h
                    edge_out[step, side, pl.ds(i, 1), :] = q[
                        step % 2, c, l, h, pl.ds(row, 1), :
                    ]

    def edge_copy(step, side):
        target = tile - 1 if side == 0 else tile + 1
        return pltpu.make_async_remote_copy(
            src_ref=edge_out.at[step, side],
            dst_ref=edge_in.at[step, 1 - side],
            send_sem=edge_send.at[step, side],
            recv_sem=edge_recv.at[step, 1 - side],
            device_id=(layout, target),
            device_id_type=MESH,
        )

    def send_edges(step):
        @pl.when(tile > 0)
        def _():
            edge_copy(step, 0).start()

        @pl.when(tile < tiles - 1)
        def _():
            edge_copy(step, 1).start()

    pl.semaphore_wait(barrier, tiles - 1 + layouts - 1)

    def gather_copy(d):
        return pltpu.make_async_remote_copy(
            src_ref=gathered.at[tile],
            dst_ref=gathered.at[tile],
            send_sem=gather_send.at[d],
            recv_sem=gather_recv.at[d],
            device_id=(layout, tile_at(d)),
            device_id_type=MESH,
        )

    for d in range(1, tiles):
        gather_copy(d).start()

    for copy in field_loads:
        copy.wait()
    pack_edge(0, 0)
    pack_edge(0, 1)
    send_edges(0)
    plane_load.wait()

    def plane_copy(d):
        return pltpu.make_async_remote_copy(
            src_ref=planes.at[layout],
            dst_ref=planes.at[layout],
            send_sem=plane_send.at[d],
            recv_sem=plane_recv.at[d],
            device_id=(layout_at(d), tile),
            device_id_type=MESH,
        )

    @pl.when(tile == 0)
    def _():
        for d in range(1, layouts):
            plane_copy(d).start()

    for copy in list_loads:
        copy.wait()
    home_slot = [jnp.int32(0)] * HOME_MOST
    home_block = [jnp.int32(0)] * HOME_MOST
    home_on = [jnp.int32(0)] * HOME_MOST
    own_site = [jnp.int32(0)] * OWN_SLOTS
    own_on = [jnp.int32(0)] * OWN_SLOTS
    for k in range(turbines):
        site = site_s[0, k]
        block = block_s[0, k]
        slot = slot_s[0, k]
        for j in range(HOME_MOST):
            hit = site == tile * HOME_MOST + j
            home_slot[j] = jnp.where(hit, slot, home_slot[j])
            home_block[j] = jnp.where(hit, block, home_block[j])
            home_on[j] = jnp.where(hit, 1, home_on[j])
        for j in range(OWN_SLOTS):
            hit = slot == tile * OWN_SLOTS + j
            own_site[j] = jnp.where(hit, site, own_site[j])
            own_on[j] = jnp.where(hit, 1, own_on[j])

    lane = lax.broadcasted_iota(jnp.int32, (ROWS, LANES), 1)
    row_id = lax.broadcasted_iota(jnp.int32, (ROWS, LANES), 0)
    lane_seg = lane // BY
    row_in = row_id % BX
    row_half = row_id // BX

    def stencil_tile(src, put, xt):
        r = first + xt * ROWS
        here = pl.ds(r, ROWS)
        below_rows = pl.ds(r - 1, ROWS)
        above_rows = pl.ds(r + 1, ROWS)
        for l in range(levels):
            centre = [[q[src, c, l, h, here, :] for h in range(halves)] for c in range(3)]
            rolled_m = [
                [pltpu.roll(centre[c][h], 1, 1) for h in range(halves)] for c in range(3)
            ]
            rolled_p = [
                [pltpu.roll(centre[c][h], LANES - 1, 1) for h in range(halves)]
                for c in range(3)
            ]
            for h in range(halves):
                plus, minus = [], []
                for c in range(3):
                    mid = centre[c][h]
                    xm = q[src, c, l, h, below_rows, :]
                    xp = q[src, c, l, h, above_rows, :]
                    ym = jnp.where(lane == 0, rolled_m[c][h - 1], rolled_m[c][h])
                    yp = jnp.where(
                        lane == LANES - 1, rolled_p[c][(h + 1) % halves], rolled_p[c][h]
                    )
                    zm = mid if l == 0 else q[src, c, l - 1, h, here, :]
                    zp = mid if l == levels - 1 else q[src, c, l + 1, h, here, :]
                    plus.append([xp - mid, yp - mid, zp - mid])
                    minus.append([mid - xm, mid - ym, mid - zm])

                def grad(c, a):
                    return plus[c][a] + minus[c][a]

                gxx, gyy, gzz = grad(0, 0), grad(1, 1), grad(2, 2)
                sxy = grad(0, 1) + grad(1, 0)
                sxz = grad(0, 2) + grad(2, 0)
                syz = grad(1, 2) + grad(2, 1)
                strain = 2.0 * (gxx * gxx + gyy * gyy + gzz * gzz)
                strain = strain + sxy * sxy + sxz * sxz + syz * syz + 4.0 * FLOOR
                nu = (0.5 * SMAG * TIME_STEP) * (strain * lax.rsqrt(strain))
                ups, downs = [], []
                for a in range(3):
                    speed = TIME_STEP * centre[a][h]
                    ups.append(nu - jnp.minimum(speed, 0.0))
                    downs.append(nu + jnp.maximum(speed, 0.0))
                for c in range(3):
                    change = ups[0] * plus[c][0] - downs[0] * minus[c][0]
                    change += ups[1] * plus[c][1] - downs[1] * minus[c][1]
                    change += ups[2] * plus[c][2] - downs[2] * minus[c][2]
                    put(c, l, h, xt, centre[c][h] + change)

    def unpack_edge(step):
        src = step % 2
        left = pl.ds(first - 1, 1)
        right = pl.ds(first + width_x, 1)

        @pl.when(tile > 0)
        def _():
            edge_copy(step, 1).wait_recv()

        def fill(side, rows, value):
            for c in range(3):
                for l in range(levels):
                    for h in range(halves):
                        q[src, c, l, h, rows, :] = value(c, l, h)

        def received(side):
            return lambda c, l, h: edge_in[
                step, side, pl.ds((c * levels + l) * halves + h, 1), :
            ]

        @pl.when(tile > 0)
        def _():
            fill(0, left, received(0))

        @pl.when(tile == 0)
        def _():
            if step == 0:
                for d in range(1, layouts):
                    pltpu.make_async_remote_copy(
                        src_ref=planes.at[layout],
                        dst_ref=planes.at[layout_at(layouts - d)],
                        send_sem=plane_send.at[d],
                        recv_sem=plane_recv.at[d],
                        device_id=(layout_at(d), tile),
                        device_id_type=MESH,
                    ).wait_recv()
            fill(
                0,
                left,
                lambda c, l, h: planes[step, c, pl.ds(l, 1), pl.ds(h * LANES, LANES)],
            )

        @pl.when(tile < tiles - 1)
        def _():
            edge_copy(step, 0).wait_recv()
            fill(1, right, received(1))

        @pl.when(tile == tiles - 1)
        def _():
            fill(
                1,
                right,
                lambda c, l, h: q[src, c, l, h, pl.ds(first + width_x - 1, 1), :],
            )

    place = []
    for j in range(HOME_MOST):
        xb = lax.div(home_block[j], jnp.int32(y_blocks))
        yb = lax.rem(home_block[j], jnp.int32(y_blocks))
        per = ROWS // BX
        place.append(
            (
                lax.div(xb, jnp.int32(per)),
                lax.rem(xb, jnp.int32(per)),
                lax.div(yb, jnp.int32(segs)),
                lax.rem(yb, jnp.int32(segs)),
            )
        )

    def total_of(cells):
        return jnp.sum(jnp.sum(cells, axis=0, keepdims=True), axis=1, keepdims=True)

    def lay_weights():
        params = []
        for j in range(HOME_MOST):
            owner = lax.div(home_slot[j], jnp.int32(OWN_SLOTS))
            which = lax.rem(home_slot[j], jnp.int32(OWN_SLOTS))
            slab = gathered[0]
            for o in range(1, tiles):
                slab = jnp.where(owner == o, gathered[o], slab)
            rows = slab[:levels]
            param = slab[OWN_SLOTS * levels : OWN_SLOTS * levels + 1]
            for i in range(1, OWN_SLOTS):
                rows = jnp.where(which == i, slab[i * levels : (i + 1) * levels], rows)
                at = OWN_SLOTS * levels + i
                param = jnp.where(which == i, slab[at : at + 1], param)
            rolled = [rows if d == 0 else pltpu.roll(rows, d * BY, 1) for d in range(segs)]
            _, x_half, _, seg = place[j]
            inside = (row_half == x_half) & (lane_seg == seg) & (home_on[j] > 0)
            square = jnp.zeros((ROWS, LANES), jnp.float32)
            for l in range(levels):
                laid = jnp.zeros((ROWS, LANES), jnp.float32)
                for d in range(segs):
                    spread = jnp.broadcast_to(rolled[d][l : l + 1, :], (ROWS, LANES))
                    pick = lax.rem(lane_seg - row_in + segs, segs) == d
                    laid = jnp.where(pick, spread, laid)
                laid = jnp.where(inside, laid, 0.0)
                weights_v[j, l] = laid
                square += laid * laid
            params.append([param[:, i : i + 1] for i in range(4)] + [total_of(square)])
        return params

    def disk(read, params):
        found = [[[None] * levels for _ in range(2)] for _ in range(HOME_MOST)]
        for xt in range(x_tiles):
            for h in range(halves):
                on = [(place[j][0] == xt) & (place[j][2] == h) for j in range(HOME_MOST)]
                for c in range(2):
                    for l in range(levels):
                        cells = read(c, l, h, xt)
                        for j in range(HOME_MOST):
                            old = found[j][c][l]
                            found[j][c][l] = (
                                cells if old is None else jnp.where(on[j], cells, old)
                            )
        totals = []
        for j in range(HOME_MOST):
            cosine, sine = params[j][:2]
            acc_u = jnp.zeros((ROWS, LANES), jnp.float32)
            acc_v = jnp.zeros((ROWS, LANES), jnp.float32)
            for l in range(levels):
                w = weights_v[j, l]
                acc_u += w * found[j][0][l]
                acc_v += w * found[j][1][l]
            totals.append(total_of(acc_u * cosine + acc_v * sine))
        return totals

    def respond(totals, params):
        results = []
        for j in range(HOME_MOST):
            cosine, sine, coef, inverse, square = params[j]
            speed = totals[j] * inverse
            pull = 0.5 * coef * jnp.abs(speed) * speed
            push = -TIME_STEP * pull
            gain = push * (cosine * cosine + sine * sine) * square
            results.append((push * cosine, push * sine, pull * speed, gain))
        return results

    def add_force(get, put, results, x_list):
        for xt in x_list:
            for h in range(halves):
                scale = []
                for j in range(HOME_MOST):
                    on = (place[j][0] == xt) & (place[j][2] == h)
                    scale.append([jnp.where(on, results[j][c], 0.0) for c in range(2)])
                for l in range(levels):
                    w = [weights_v[j, l] for j in range(HOME_MOST)]
                    for c in range(2):
                        force = scale[0][c] * w[0]
                        for j in range(1, HOME_MOST):
                            force += scale[j][c] * w[j]
                        put(c, l, h, xt, get(c, l, h, xt) + force)

    def power_copy(d):
        return pltpu.make_async_remote_copy(
            src_ref=powers.at[tile],
            dst_ref=powers.at[tile],
            send_sem=power_send.at[d],
            recv_sem=power_recv.at[d],
            device_id=(layout, tile_at(d)),
            device_id_type=MESH,
        )

    def access(step):
        dst = (step + 1) % 2

        def where_at(c, l, h, xt):
            if step == steps - 1:
                return out_ref, (0, c, l, pl.ds(xt * ROWS, ROWS), pl.ds(h * LANES, LANES))
            return q, (dst, c, l, h, pl.ds(first + xt * ROWS, ROWS), slice(None))

        def get(*at):
            ref, index = where_at(*at)
            return ref[index]

        def put(c, l, h, xt, value):
            ref, index = where_at(c, l, h, xt)
            ref[index] = value

        return get, put

    power_row = jnp.zeros((1, LANES), jnp.float32)
    def add_power(row, results):
        for j in range(HOME_MOST):
            row = row + jnp.where(lane1 == j, results[j][2], 0.0)
        return row

    def send_powers(row):
        powers[tile] = row * (1.0 / steps)
        for d in range(1, tiles):
            power_copy(d).start()

    def wait_gather():
        for d in range(1, tiles):
            pltpu.make_async_remote_copy(
                src_ref=gathered.at[tile],
                dst_ref=gathered.at[tile_at(tiles - d)],
                send_sem=gather_send.at[d],
                recv_sem=gather_recv.at[d],
                device_id=(layout, tile_at(d)),
                device_id_type=MESH,
            ).wait_recv()

    outer = (0, x_tiles - 1)
    inner = range(1, x_tiles - 1)
    params, results = None, None
    for step in range(steps):
        src = step % 2
        get, put = access(step)
        lax.fori_loop(
            1, x_tiles - 1, lambda xt, c: (stencil_tile(src, put, xt), c)[1], 0
        )
        unpack_edge(step)
        lax.fori_loop(
            0,
            2,
            lambda i, c: (stencil_tile(src, put, i * (x_tiles - 1)), c)[1],
            0,
        )
        if step == 0:
            wait_gather()
            params = lay_weights()
            now = disk(
                lambda c, l, h, xt: q[src, c, l, h, pl.ds(first + xt * ROWS, ROWS), :],
                params,
            )
            results = respond(now, params)
            power_row = add_power(power_row, results)
            if steps == 1:
                send_powers(power_row)
        if step == steps - 1:
            add_force(get, put, results, range(x_tiles))
            continue
        ahead = disk(get, params)
        ahead = [ahead[j] + results[j][3] for j in range(HOME_MOST)]
        later = respond(ahead, params)
        power_row = add_power(power_row, later)
        add_force(get, put, results, outer)
        pack_edge(step + 1, 0)
        pack_edge(step + 1, 1)
        send_edges(step + 1)
        if step == steps - 2:
            send_powers(power_row)
        add_force(get, put, results, inner)
        results = later

    for d in range(1, tiles):
        pltpu.make_async_remote_copy(
            src_ref=powers.at[tile],
            dst_ref=powers.at[tile_at(tiles - d)],
            send_sem=power_send.at[d],
            recv_sem=power_recv.at[d],
            device_id=(layout, tile_at(d)),
            device_id_type=MESH,
        ).wait_recv()
    lane_out = lax.broadcasted_iota(jnp.int32, (1, OWN_SLOTS), 1)
    answer = jnp.zeros((1, OWN_SLOTS), jnp.float32)
    rows_in = [powers[o] for o in range(tiles)]
    for j in range(OWN_SLOTS):
        home = lax.div(own_site[j], jnp.int32(HOME_MOST))
        which = lax.rem(own_site[j], jnp.int32(HOME_MOST))
        row = rows_in[0]
        for o in range(1, tiles):
            row = jnp.where(home == o, rows_in[o], row)
        value = jnp.sum(jnp.where(lane1 == which, row, 0.0), axis=1, keepdims=True)
        value = jnp.where(own_on[j] > 0, value, 0.0)
        answer = jnp.where(lane_out == j, value, answer)
    power_ref[...] = answer

    for step in range(steps):
        @pl.when(tile > 0)
        def _():
            edge_copy(step, 0).wait_send()

        @pl.when(tile < tiles - 1)
        def _():
            edge_copy(step, 1).wait_send()

    @pl.when(tile == 0)
    def _():
        for d in range(1, layouts):
            plane_copy(d).wait_send()

    for d in range(1, tiles):
        gather_copy(d).wait_send()
        power_copy(d).wait_send()


def solution(mesh):
    tiles = mesh.shape["tile"]
    layouts = mesh.shape["layout"]

    def local(velocity, inflow, turbine_site, turbine_block, turbine_slot, smear, yaw, thrust_coef):
        _, _, levels, width_x, width_y = velocity.shape
        halves = width_y // LANES
        turbines = turbine_site.shape[1]
        edge_rows = 3 * levels * halves
        f32 = jnp.float32
        slab = -(-OWN_SLOTS * (levels + 1) // ROWS) * ROWS
        dma = pltpu.SemaphoreType.DMA
        inside = pl.BlockSpec(memory_space=pltpu.VMEM)
        return pl.pallas_call(
            functools.partial(kernel, tiles, layouts, levels, width_x, halves, turbines),
            out_shape=(
                pltpu.VMEM(velocity.shape, f32),
                pltpu.VMEM(yaw.shape, f32),
            ),
            in_specs=[pl.BlockSpec(memory_space=pltpu.HBM)] * 8,
            out_specs=(inside, inside),
            scratch_shapes=[
                pltpu.VMEM((2, 3, levels, halves, width_x + 2 * ROWS, LANES), f32),
                pltpu.SMEM((1, turbines), jnp.int32),
                pltpu.SMEM((1, turbines), jnp.int32),
                pltpu.SMEM((1, turbines), jnp.int32),
                pltpu.VMEM(smear.shape[1:], f32),
                pltpu.VMEM(yaw.shape, f32),
                pltpu.VMEM(yaw.shape, f32),
                pltpu.VMEM((tiles, slab, LANES), f32),
                pltpu.VMEM((HOME_MOST, levels, ROWS, LANES), f32),
                pltpu.VMEM((layouts, 3, levels, width_y), f32),
                pltpu.VMEM((layouts, 2, edge_rows, LANES), f32),
                pltpu.VMEM((layouts, 2, edge_rows, LANES), f32),
                pltpu.VMEM((tiles, 1, LANES), f32),
                dma((7 + halves,)),
                dma((tiles,)),
                dma((tiles,)),
                dma((layouts,)),
                dma((layouts,)),
                dma((layouts, 2)),
                dma((layouts, 2)),
                dma((tiles,)),
                dma((tiles,)),
            ],
            compiler_params=pltpu.CompilerParams(
                collective_id=0, has_side_effects=True, vmem_limit_bytes=60 * 1024 * 1024
            ),
        )(
            velocity, inflow, turbine_site, turbine_block, turbine_slot,
            jnp.transpose(smear, (1, 0, 2)), yaw, thrust_coef,
        )

    in_specs = (
        P("layout", None, None, "tile", None),
        P("layout", None, None, None),
        P("layout", None),
        P("layout", None),
        P("layout", None),
        P("layout", "tile", None),
        P("layout", "tile"),
        P("layout", "tile"),
    )
    out_specs = (P("layout", None, None, "tile", None), P("layout", "tile"))
    return jax.shard_map(local, mesh=mesh, in_specs=in_specs, out_specs=out_specs, check_vma=False)
```

```python
import functools

import jax
import jax.numpy as jnp
from jax import lax
from jax.experimental import pallas as pl
from jax.experimental.pallas import tpu as pltpu
from jax.sharding import PartitionSpec as P

BX = 4
BY = 32
HOME_MOST = 3
OWN_SLOTS = 3
LANES = 128
ROWS = 8

TIME_STEP = 0.1
SMAG = 0.0256
FLOOR = 0.01

MESH = pl.DeviceIdType.MESH


def kernel(
    tiles, layouts, levels, width_x, halves, turbines,
    vel_ref, inflow_ref, site_ref, block_ref, slot_ref, smear_ref, yaw_ref, coef_ref,
    out_ref, power_ref,
    q, site_s, block_s, slot_s, smear_v, yaw_v, coef_v, gathered, weights_v,
    planes, edge_out, edge_in, powers,
    local_sem, gather_send, gather_recv, plane_send, plane_recv,
    edge_send, edge_recv, power_send, power_recv,
):
    tile = lax.axis_index("tile")
    layout = lax.axis_index("layout")
    steps = layouts
    fields = 3 * levels
    x_tiles = width_x // ROWS
    first = ROWS
    y_blocks = halves * LANES // BY
    segs = LANES // BY

    def tile_at(distance):
        return lax.rem(tile + distance, tiles)

    def layout_at(distance):
        return lax.rem(layout + distance, layouts)

    barrier = pltpu.get_barrier_semaphore()
    for d in range(1, tiles):
        pl.semaphore_signal(
            barrier, inc=1, device_id=(layout, tile_at(d)), device_id_type=MESH
        )
    for d in range(1, layouts):
        pl.semaphore_signal(
            barrier, inc=1, device_id=(layout_at(d), tile), device_id_type=MESH
        )

    loads = [
        pltpu.make_async_copy(smear_ref.at[:, 0], smear_v, local_sem.at[0]),
        pltpu.make_async_copy(yaw_ref, yaw_v, local_sem.at[1]),
        pltpu.make_async_copy(coef_ref, coef_v, local_sem.at[2]),
    ]
    field_loads = [
        pltpu.make_async_copy(
            vel_ref.at[0, :, :, :, pl.ds(h * LANES, LANES)],
            q.at[0, :, :, h, pl.ds(first, width_x), :],
            local_sem.at[3 + h],
        )
        for h in range(halves)
    ]
    base = 3 + halves
    plane_load = pltpu.make_async_copy(
        inflow_ref.at[0], planes.at[layout], local_sem.at[base]
    )
    list_loads = [
        pltpu.make_async_copy(site_ref, site_s, local_sem.at[base + 1]),
        pltpu.make_async_copy(block_ref, block_s, local_sem.at[base + 2]),
        pltpu.make_async_copy(slot_ref, slot_s, local_sem.at[base + 3]),
    ]
    for copy in loads + field_loads + [plane_load] + list_loads:
        copy.start()

    for copy in loads:
        copy.wait()
    lane1 = lax.broadcasted_iota(jnp.int32, (1, LANES), 1)
    for j in range(OWN_SLOTS):
        total = jnp.zeros((1, 1), jnp.float32)
        for l in range(levels):
            row = smear_v[pl.ds(j, 1), pl.ds(l * LANES, LANES)]
            gathered[tile, pl.ds(j * levels + l, 1), :] = row
            total = total + jnp.sum(row, axis=1, keepdims=True)
        angle = yaw_v[:, j : j + 1]
        packed = jnp.where(lane1 == 0, jnp.cos(angle), 0.0)
        packed = jnp.where(lane1 == 1, jnp.sin(angle), packed)
        packed = jnp.where(lane1 == 2, coef_v[:, j : j + 1], packed)
        packed = jnp.where(lane1 == 3, 1.0 / total, packed)
        gathered[tile, pl.ds(OWN_SLOTS * levels + j, 1), :] = packed

    def pack_edge(step, side):
        row = first if side == 0 else first + width_x - 1
        for c in range(3):
            for l in range(levels):
                for h in range(halves):
                    i = (c * levels + l) * halves + h
                    edge_out[step, side, pl.ds(i, 1), :] = q[
                        step % 2, c, l, h, pl.ds(row, 1), :
                    ]

    def edge_copy(step, side):
        target = tile - 1 if side == 0 else tile + 1
        return pltpu.make_async_remote_copy(
            src_ref=edge_out.at[step, side],
            dst_ref=edge_in.at[step, 1 - side],
            send_sem=edge_send.at[step, side],
            recv_sem=edge_recv.at[step, 1 - side],
            device_id=(layout, target),
            device_id_type=MESH,
        )

    def send_edges(step):
        @pl.when(tile > 0)
        def _():
            edge_copy(step, 0).start()

        @pl.when(tile < tiles - 1)
        def _():
            edge_copy(step, 1).start()

    pl.semaphore_wait(barrier, tiles - 1 + layouts - 1)

    def gather_copy(d):
        return pltpu.make_async_remote_copy(
            src_ref=gathered.at[tile],
            dst_ref=gathered.at[tile],
            send_sem=gather_send.at[d],
            recv_sem=gather_recv.at[d],
            device_id=(layout, tile_at(d)),
            device_id_type=MESH,
        )

    for d in range(1, tiles):
        gather_copy(d).start()

    for copy in field_loads:
        copy.wait()
    pack_edge(0, 0)
    pack_edge(0, 1)
    send_edges(0)
    plane_load.wait()

    def plane_copy(d):
        return pltpu.make_async_remote_copy(
            src_ref=planes.at[layout],
            dst_ref=planes.at[layout],
            send_sem=plane_send.at[d],
            recv_sem=plane_recv.at[d],
            device_id=(layout_at(d), tile),
            device_id_type=MESH,
        )

    @pl.when(tile == 0)
    def _():
        for d in range(1, layouts):
            plane_copy(d).start()

    for copy in list_loads:
        copy.wait()
    home_slot = [jnp.int32(0)] * HOME_MOST
    home_block = [jnp.int32(0)] * HOME_MOST
    home_on = [jnp.int32(0)] * HOME_MOST
    own_site = [jnp.int32(0)] * OWN_SLOTS
    own_on = [jnp.int32(0)] * OWN_SLOTS
    for k in range(turbines):
        site = site_s[0, k]
        block = block_s[0, k]
        slot = slot_s[0, k]
        for j in range(HOME_MOST):
            hit = site == tile * HOME_MOST + j
            home_slot[j] = jnp.where(hit, slot, home_slot[j])
            home_block[j] = jnp.where(hit, block, home_block[j])
            home_on[j] = jnp.where(hit, 1, home_on[j])
        for j in range(OWN_SLOTS):
            hit = slot == tile * OWN_SLOTS + j
            own_site[j] = jnp.where(hit, site, own_site[j])
            own_on[j] = jnp.where(hit, 1, own_on[j])

    lane = lax.broadcasted_iota(jnp.int32, (ROWS, LANES), 1)
    row_id = lax.broadcasted_iota(jnp.int32, (ROWS, LANES), 0)
    lane_seg = lane // BY
    row_in = row_id % BX
    row_half = row_id // BX

    def stencil_tile(src, put, xt):
        r = first + xt * ROWS
        here = pl.ds(r, ROWS)
        below_rows = pl.ds(r - 1, ROWS)
        above_rows = pl.ds(r + 1, ROWS)
        for l in range(levels):
            centre = [[q[src, c, l, h, here, :] for h in range(halves)] for c in range(3)]
            rolled_m = [
                [pltpu.roll(centre[c][h], 1, 1) for h in range(halves)] for c in range(3)
            ]
            rolled_p = [
                [pltpu.roll(centre[c][h], LANES - 1, 1) for h in range(halves)]
                for c in range(3)
            ]
            for h in range(halves):
                plus, minus = [], []
                for c in range(3):
                    mid = centre[c][h]
                    xm = q[src, c, l, h, below_rows, :]
                    xp = q[src, c, l, h, above_rows, :]
                    ym = jnp.where(lane == 0, rolled_m[c][h - 1], rolled_m[c][h])
                    yp = jnp.where(
                        lane == LANES - 1, rolled_p[c][(h + 1) % halves], rolled_p[c][h]
                    )
                    zm = mid if l == 0 else q[src, c, l - 1, h, here, :]
                    zp = mid if l == levels - 1 else q[src, c, l + 1, h, here, :]
                    plus.append([xp - mid, yp - mid, zp - mid])
                    minus.append([mid - xm, mid - ym, mid - zm])

                def grad(c, a):
                    return plus[c][a] + minus[c][a]

                gxx, gyy, gzz = grad(0, 0), grad(1, 1), grad(2, 2)
                sxy = grad(0, 1) + grad(1, 0)
                sxz = grad(0, 2) + grad(2, 0)
                syz = grad(1, 2) + grad(2, 1)
                strain = 2.0 * (gxx * gxx + gyy * gyy + gzz * gzz)
                strain = strain + sxy * sxy + sxz * sxz + syz * syz + 4.0 * FLOOR
                nu = (0.5 * SMAG * TIME_STEP) * (strain * lax.rsqrt(strain))
                ups, downs = [], []
                for a in range(3):
                    speed = TIME_STEP * centre[a][h]
                    ups.append(nu - jnp.minimum(speed, 0.0))
                    downs.append(nu + jnp.maximum(speed, 0.0))
                for c in range(3):
                    change = ups[0] * plus[c][0] - downs[0] * minus[c][0]
                    change += ups[1] * plus[c][1] - downs[1] * minus[c][1]
                    change += ups[2] * plus[c][2] - downs[2] * minus[c][2]
                    put(c, l, h, xt, centre[c][h] + change)

    def unpack_edge(step):
        src = step % 2
        left = pl.ds(first - 1, 1)
        right = pl.ds(first + width_x, 1)

        @pl.when(tile > 0)
        def _():
            edge_copy(step, 1).wait_recv()

        def fill(side, rows, value):
            for c in range(3):
                for l in range(levels):
                    for h in range(halves):
                        q[src, c, l, h, rows, :] = value(c, l, h)

        def received(side):
            return lambda c, l, h: edge_in[
                step, side, pl.ds((c * levels + l) * halves + h, 1), :
            ]

        @pl.when(tile > 0)
        def _():
            fill(0, left, received(0))

        @pl.when(tile == 0)
        def _():
            if step == 0:
                for d in range(1, layouts):
                    pltpu.make_async_remote_copy(
                        src_ref=planes.at[layout],
                        dst_ref=planes.at[layout_at(layouts - d)],
                        send_sem=plane_send.at[d],
                        recv_sem=plane_recv.at[d],
                        device_id=(layout_at(d), tile),
                        device_id_type=MESH,
                    ).wait_recv()
            fill(
                0,
                left,
                lambda c, l, h: planes[step, c, pl.ds(l, 1), pl.ds(h * LANES, LANES)],
            )

        @pl.when(tile < tiles - 1)
        def _():
            edge_copy(step, 0).wait_recv()
            fill(1, right, received(1))

        @pl.when(tile == tiles - 1)
        def _():
            fill(
                1,
                right,
                lambda c, l, h: q[src, c, l, h, pl.ds(first + width_x - 1, 1), :],
            )

    place = []
    for j in range(HOME_MOST):
        xb = lax.div(home_block[j], jnp.int32(y_blocks))
        yb = lax.rem(home_block[j], jnp.int32(y_blocks))
        per = ROWS // BX
        place.append(
            (
                lax.div(xb, jnp.int32(per)),
                lax.rem(xb, jnp.int32(per)),
                lax.div(yb, jnp.int32(segs)),
                lax.rem(yb, jnp.int32(segs)),
            )
        )

    def total_of(cells):
        return jnp.sum(jnp.sum(cells, axis=0, keepdims=True), axis=1, keepdims=True)

    def lay_weights():
        params = []
        for j in range(HOME_MOST):
            owner = lax.div(home_slot[j], jnp.int32(OWN_SLOTS))
            which = lax.rem(home_slot[j], jnp.int32(OWN_SLOTS))
            slab = gathered[0]
            for o in range(1, tiles):
                slab = jnp.where(owner == o, gathered[o], slab)
            rows = slab[:levels]
            param = slab[OWN_SLOTS * levels : OWN_SLOTS * levels + 1]
            for i in range(1, OWN_SLOTS):
                rows = jnp.where(which == i, slab[i * levels : (i + 1) * levels], rows)
                at = OWN_SLOTS * levels + i
                param = jnp.where(which == i, slab[at : at + 1], param)
            rolled = [rows if d == 0 else pltpu.roll(rows, d * BY, 1) for d in range(segs)]
            _, x_half, _, seg = place[j]
            inside = (row_half == x_half) & (lane_seg == seg) & (home_on[j] > 0)
            square = jnp.zeros((ROWS, LANES), jnp.float32)
            for l in range(levels):
                laid = jnp.zeros((ROWS, LANES), jnp.float32)
                for d in range(segs):
                    spread = jnp.broadcast_to(rolled[d][l : l + 1, :], (ROWS, LANES))
                    pick = lax.rem(lane_seg - row_in + segs, segs) == d
                    laid = jnp.where(pick, spread, laid)
                laid = jnp.where(inside, laid, 0.0)
                weights_v[j, l] = laid
                square += laid * laid
            params.append([param[:, i : i + 1] for i in range(4)] + [total_of(square)])
        return params

    def disk(read, params):
        found = [[[None] * levels for _ in range(2)] for _ in range(HOME_MOST)]
        for xt in range(x_tiles):
            for h in range(halves):
                on = [(place[j][0] == xt) & (place[j][2] == h) for j in range(HOME_MOST)]
                for c in range(2):
                    for l in range(levels):
                        cells = read(c, l, h, xt)
                        for j in range(HOME_MOST):
                            old = found[j][c][l]
                            found[j][c][l] = (
                                cells if old is None else jnp.where(on[j], cells, old)
                            )
        totals = []
        for j in range(HOME_MOST):
            cosine, sine = params[j][:2]
            acc_u = jnp.zeros((ROWS, LANES), jnp.float32)
            acc_v = jnp.zeros((ROWS, LANES), jnp.float32)
            for l in range(levels):
                w = weights_v[j, l]
                acc_u += w * found[j][0][l]
                acc_v += w * found[j][1][l]
            totals.append(total_of(acc_u * cosine + acc_v * sine))
        return totals

    def respond(totals, params):
        results = []
        for j in range(HOME_MOST):
            cosine, sine, coef, inverse, square = params[j]
            speed = totals[j] * inverse
            pull = 0.5 * coef * jnp.abs(speed) * speed
            push = -TIME_STEP * pull
            gain = push * (cosine * cosine + sine * sine) * square
            results.append((push * cosine, push * sine, pull * speed, gain))
        return results

    def add_force(get, put, results, x_list):
        for xt in x_list:
            for h in range(halves):
                scale = []
                for j in range(HOME_MOST):
                    on = (place[j][0] == xt) & (place[j][2] == h)
                    scale.append([jnp.where(on, results[j][c], 0.0) for c in range(2)])
                for l in range(levels):
                    w = [weights_v[j, l] for j in range(HOME_MOST)]
                    for c in range(2):
                        force = scale[0][c] * w[0]
                        for j in range(1, HOME_MOST):
                            force += scale[j][c] * w[j]
                        put(c, l, h, xt, get(c, l, h, xt) + force)

    def power_copy(d):
        return pltpu.make_async_remote_copy(
            src_ref=powers.at[tile],
            dst_ref=powers.at[tile],
            send_sem=power_send.at[d],
            recv_sem=power_recv.at[d],
            device_id=(layout, tile_at(d)),
            device_id_type=MESH,
        )

    def access(step):
        dst = (step + 1) % 2

        def where_at(c, l, h, xt):
            if step == steps - 1:
                return out_ref, (0, c, l, pl.ds(xt * ROWS, ROWS), pl.ds(h * LANES, LANES))
            return q, (dst, c, l, h, pl.ds(first + xt * ROWS, ROWS), slice(None))

        def get(*at):
            ref, index = where_at(*at)
            return ref[index]

        def put(c, l, h, xt, value):
            ref, index = where_at(c, l, h, xt)
            ref[index] = value

        return get, put

    power_row = jnp.zeros((1, LANES), jnp.float32)
    def add_power(row, results):
        for j in range(HOME_MOST):
            row = row + jnp.where(lane1 == j, results[j][2], 0.0)
        return row

    def send_powers(row):
        powers[tile] = row * (1.0 / steps)
        for d in range(1, tiles):
            power_copy(d).start()

    def wait_gather():
        for d in range(1, tiles):
            pltpu.make_async_remote_copy(
                src_ref=gathered.at[tile],
                dst_ref=gathered.at[tile_at(tiles - d)],
                send_sem=gather_send.at[d],
                recv_sem=gather_recv.at[d],
                device_id=(layout, tile_at(d)),
                device_id_type=MESH,
            ).wait_recv()

    outer = (0, x_tiles - 1)
    inner = range(1, x_tiles - 1)
    params, results = None, None
    for step in range(steps):
        src = step % 2
        get, put = access(step)
        lax.fori_loop(
            1, x_tiles - 1, lambda xt, c: (stencil_tile(src, put, xt), c)[1], 0
        )
        unpack_edge(step)
        lax.fori_loop(
            0,
            2,
            lambda i, c: (stencil_tile(src, put, i * (x_tiles - 1)), c)[1],
            0,
        )
        if step == 0:
            wait_gather()
            params = lay_weights()
            now = disk(
                lambda c, l, h, xt: q[src, c, l, h, pl.ds(first + xt * ROWS, ROWS), :],
                params,
            )
            results = respond(now, params)
            power_row = add_power(power_row, results)
            if steps == 1:
                send_powers(power_row)
        if step == steps - 1:
            add_force(get, put, results, range(x_tiles))
            continue
        ahead = disk(get, params)
        ahead = [ahead[j] + results[j][3] for j in range(HOME_MOST)]
        later = respond(ahead, params)
        power_row = add_power(power_row, later)
        if step == steps - 2:
            send_powers(power_row)
        add_force(get, put, results, outer)
        pack_edge(step + 1, 0)
        pack_edge(step + 1, 1)
        send_edges(step + 1)
        add_force(get, put, results, inner)
        results = later

    for d in range(1, tiles):
        pltpu.make_async_remote_copy(
            src_ref=powers.at[tile],
            dst_ref=powers.at[tile_at(tiles - d)],
            send_sem=power_send.at[d],
            recv_sem=power_recv.at[d],
            device_id=(layout, tile_at(d)),
            device_id_type=MESH,
        ).wait_recv()
    lane_out = lax.broadcasted_iota(jnp.int32, (1, OWN_SLOTS), 1)
    answer = jnp.zeros((1, OWN_SLOTS), jnp.float32)
    rows_in = [powers[o] for o in range(tiles)]
    for j in range(OWN_SLOTS):
        home = lax.div(own_site[j], jnp.int32(HOME_MOST))
        which = lax.rem(own_site[j], jnp.int32(HOME_MOST))
        row = rows_in[0]
        for o in range(1, tiles):
            row = jnp.where(home == o, rows_in[o], row)
        value = jnp.sum(jnp.where(lane1 == which, row, 0.0), axis=1, keepdims=True)
        value = jnp.where(own_on[j] > 0, value, 0.0)
        answer = jnp.where(lane_out == j, value, answer)
    power_ref[...] = answer

    for step in range(steps):
        @pl.when(tile > 0)
        def _():
            edge_copy(step, 0).wait_send()

        @pl.when(tile < tiles - 1)
        def _():
            edge_copy(step, 1).wait_send()

    @pl.when(tile == 0)
    def _():
        for d in range(1, layouts):
            plane_copy(d).wait_send()

    for d in range(1, tiles):
        gather_copy(d).wait_send()
        power_copy(d).wait_send()


def solution(mesh):
    tiles = mesh.shape["tile"]
    layouts = mesh.shape["layout"]

    def local(velocity, inflow, turbine_site, turbine_block, turbine_slot, smear, yaw, thrust_coef):
        _, _, levels, width_x, width_y = velocity.shape
        halves = width_y // LANES
        turbines = turbine_site.shape[1]
        edge_rows = 3 * levels * halves
        f32 = jnp.float32
        slab = -(-OWN_SLOTS * (levels + 1) // ROWS) * ROWS
        dma = pltpu.SemaphoreType.DMA
        inside = pl.BlockSpec(memory_space=pltpu.VMEM)
        return pl.pallas_call(
            functools.partial(kernel, tiles, layouts, levels, width_x, halves, turbines),
            out_shape=(
                pltpu.VMEM(velocity.shape, f32),
                pltpu.VMEM(yaw.shape, f32),
            ),
            in_specs=[pl.BlockSpec(memory_space=pltpu.HBM)] * 8,
            out_specs=(inside, inside),
            scratch_shapes=[
                pltpu.VMEM((2, 3, levels, halves, width_x + 2 * ROWS, LANES), f32),
                pltpu.SMEM((1, turbines), jnp.int32),
                pltpu.SMEM((1, turbines), jnp.int32),
                pltpu.SMEM((1, turbines), jnp.int32),
                pltpu.VMEM(smear.shape[1:], f32),
                pltpu.VMEM(yaw.shape, f32),
                pltpu.VMEM(yaw.shape, f32),
                pltpu.VMEM((tiles, slab, LANES), f32),
                pltpu.VMEM((HOME_MOST, levels, ROWS, LANES), f32),
                pltpu.VMEM((layouts, 3, levels, width_y), f32),
                pltpu.VMEM((layouts, 2, edge_rows, LANES), f32),
                pltpu.VMEM((layouts, 2, edge_rows, LANES), f32),
                pltpu.VMEM((tiles, 1, LANES), f32),
                dma((7 + halves,)),
                dma((tiles,)),
                dma((tiles,)),
                dma((layouts,)),
                dma((layouts,)),
                dma((layouts, 2)),
                dma((layouts, 2)),
                dma((tiles,)),
                dma((tiles,)),
            ],
            compiler_params=pltpu.CompilerParams(
                collective_id=0, has_side_effects=True, vmem_limit_bytes=60 * 1024 * 1024
            ),
        )(
            velocity, inflow, turbine_site, turbine_block, turbine_slot,
            jnp.transpose(smear, (1, 0, 2)), yaw, thrust_coef,
        )

    in_specs = (
        P("layout", None, None, "tile", None),
        P("layout", None, None, None),
        P("layout", None),
        P("layout", None),
        P("layout", None),
        P("layout", "tile", None),
        P("layout", "tile"),
        P("layout", "tile"),
    )
    out_specs = (P("layout", None, None, "tile", None), P("layout", "tile"))
    return jax.shard_map(local, mesh=mesh, in_specs=in_specs, out_specs=out_specs, check_vma=False)
```
